256 devices in a mesh: sect: 2 (over core), vocab: 16 (over z_lo, x), seq: 8 (over z_hi, y).
Axes of the slice: x: 4, y: 4, z: 8 (z_hi: 2, z_lo: 4; z = z_hi * 4 + z_lo), core: 2. Of those that a mesh axis runs over, the one named last changes fastest.
Arguments:
- hidden: bfloat16 [1024, 5120], P('seq'), may hold values from -29 to 29
- head_weight: bfloat16 [5120, 77824], P('seq', ('vocab', 'sect'))
- teacher_logits: bfloat16 [1024, 77824], P(('seq', 'sect'), 'vocab'), may hold values from -460 to 460
- sampled_ids: int32 [1024], P('seq'), may hold values from 0 to 77823
- behaviour_logprob: float32 [1024], P('seq'), may hold values from -18 to 0
- valid_mask: int32 [1024], P('seq'), may hold values from 0 to 1, as said below
Outputs:
- logit_grad: bfloat16 [1024, 77824], P('seq', ('vocab', 'sect'))
- hidden_grad: bfloat16 [1024, 5120], P('seq')
- weight_grad: bfloat16 [5120, 77824], P('seq', ('vocab', 'sect'))
- entropy: float32 [1024], P('seq')
- token_kl: float32 [1024], P('seq')
The draws below stay inside these ranges and needn't reach their ends.
Inputs may be any that keep to these rules, and one draw needn't show every extreme that they name: `valid_mask`: the last token of the micro-batch is valid.
All inputs are finite; a program needn't handle non-finite values.
Results may differ from the reference program's by a relative error of at most 0.005.
Values may be sent and summed in bfloat16 or wider, within the bound.
No kernel may reach another device: no remote copies, remote signals or barrier semaphores. Data moves between devices by JAX's collectives and lax.ppermute only.
A program may use at most 128 MiB of HBM per device.

```python
import math
import jax
import jax.numpy as jnp
from jax import lax

DS = 5120
V = 77824
TOK = 1024


def draw_hidden(key, part):
    key = jax.random.fold_in(key, 12)
    keys = jax.random.split(key, 2)
    row_scale = jnp.exp(jax.random.uniform(keys[0], (TOK, 1), jnp.float32, math.log(0.06), math.log(0.6)))
    values = jnp.clip(jax.random.normal(keys[1], (TOK, DS), jnp.float32), -4.0, 4.0) * row_scale
    return values.astype(jnp.bfloat16)


def draw_head_weight(key, part):
    key = jax.random.fold_in(key, 11)
    keys = jax.random.split(key, 2)
    position = jnp.arange(V, dtype=jnp.float32) / V
    column_scale = jnp.exp(jax.random.uniform(keys[0], (V,), jnp.float32, math.log(0.6), math.log(1.6))) * (1.0 + position) * (1.0 / math.sqrt(DS))
    values = jnp.clip(jax.random.normal(keys[1], (DS, V), jnp.float32), -4.0, 4.0) * column_scale[None, :]
    return values.astype(jnp.bfloat16)


def draw_teacher_logits(key, part):
    key = jax.random.fold_in(key, 13)
    keys = jax.random.split(key, 3)
    position = jnp.arange(V, dtype=jnp.float32)[None, :] / V
    column_scale = jnp.exp(jax.random.uniform(keys[0], (1, V), jnp.float32, math.log(0.7), math.log(1.4))) * (1.0 + 2.0 * position)
    row_scale = jnp.exp(jax.random.uniform(keys[1], (TOK, 1), jnp.float32, 0.0, math.log(3.0))) * 1.5
    values = jnp.clip(jax.random.normal(keys[2], (TOK, V), jnp.float32), -4.0, 4.0) * row_scale * column_scale
    return values.astype(jnp.bfloat16)


def draw_behaviour_logprob(key, part):
    key = jax.random.fold_in(key, 15)
    values = jax.random.uniform(key, (TOK,), jnp.float32, -3.0, 0.0)
    return values.astype(jnp.float32)


def draw_valid_mask(key, part):
    key = jax.random.fold_in(key, 14)
    position = jnp.arange(TOK, dtype=jnp.int32)
    levels = jax.random.randint(key, (TOK,), 0, 100)
    valid = (levels * TOK < 25 * TOK + 70 * position).astype(jnp.int32)
    return jnp.where(position == TOK - 1, 1, valid).astype(jnp.int32)


def place_ends(values, own_key, least, top_value):
    index_at = [jax.random.randint(jax.random.fold_in(own_key, axis), (), 0, length) for axis, length in enumerate(values.shape)]
    main_axis = values.shape.index(max(values.shape))
    next_to = index_at[:main_axis] + [(index_at[main_axis] + 1) % values.shape[main_axis]] + index_at[main_axis + 1:]
    return values.at[tuple(index_at)].set(least).at[tuple(next_to)].set(top_value)


def setup_inputs(seed: int = 0) -> dict:
    seeds = jax.random.split(jax.random.key(seed), 7)
    hidden = draw_hidden(jax.random.fold_in(seeds[6], 71), 0)
    head_weight = draw_head_weight(jax.random.fold_in(seeds[6], 71), 0)
    teacher_logits = draw_teacher_logits(jax.random.fold_in(seeds[6], 71), 0)
    sampled_ids = place_ends(jax.random.randint(seeds[3], (TOK,), 0, V), jax.random.fold_in(seeds[3], 1), 0, V - 1).astype(jnp.int32)
    behaviour_logprob = draw_behaviour_logprob(jax.random.fold_in(seeds[6], 71), 0)
    valid_mask = draw_valid_mask(jax.random.fold_in(seeds[6], 71), 0)
    return {"hidden": hidden, "head_weight": head_weight, "teacher_logits": teacher_logits, "sampled_ids": sampled_ids, "behaviour_logprob": behaviour_logprob, "valid_mask": valid_mask}


CLIP_RATIO = 2.0


def reference(hidden, head_weight, teacher_logits, sampled_ids, behaviour_logprob, valid_mask):
    logits = jnp.dot(hidden, head_weight, preferred_element_type=jnp.float32)
    teacher = teacher_logits.astype(jnp.float32)
    student_max = jnp.max(logits, axis=1, keepdims=True)
    teacher_max = jnp.max(teacher, axis=1, keepdims=True)
    powers = jnp.exp(logits - student_max)
    student_sum = jnp.sum(powers, axis=1, keepdims=True)
    shifted_sum = jnp.sum(powers * (logits - student_max), axis=1, keepdims=True)
    teacher_mix = jnp.sum(powers * teacher, axis=1, keepdims=True)
    teacher_sum = jnp.sum(jnp.exp(teacher - teacher_max), axis=1, keepdims=True)
    sampled_logit = jnp.take_along_axis(logits, sampled_ids[:, None].astype(jnp.int32), axis=1)
    log_student = jnp.log(student_sum)
    student_lse = student_max + log_student
    teacher_lse = teacher_max + jnp.log(teacher_sum)
    entropy = log_student - shifted_sum / student_sum
    token_kl = shifted_sum / student_sum - log_student - teacher_mix / student_sum + teacher_lse
    ratio_weight = jnp.minimum(jnp.exp(sampled_logit - student_lse - behaviour_logprob[:, None]), CLIP_RATIO)
    valid_rows = valid_mask.astype(jnp.float32)[:, None]
    valid_count = jnp.sum(valid_rows)
    row_factor = valid_rows * ratio_weight / valid_count
    logit_grad = (row_factor * (powers / student_sum) * ((logits - student_lse) - (teacher - teacher_lse) - token_kl)).astype(jnp.bfloat16)
    weight_grad = lax.dot_general(hidden, logit_grad, (((0,), (0,)), ((), ())), preferred_element_type=jnp.float32).astype(jnp.bfloat16)
    hidden_grad = lax.dot_general(logit_grad, head_weight, (((1,), (1,)), ((), ())), preferred_element_type=jnp.float32).astype(jnp.bfloat16)
    return logit_grad, hidden_grad, weight_grad, entropy[:, 0], token_kl[:, 0]
```

```python
import jax
import jax.numpy as jnp
from jax import lax
from jax.sharding import Mesh, PartitionSpec as P

CLIP_RATIO = 2.0
AXES = ("sect", "z_lo", "x", "z_hi", "y")
SIZES = (2, 4, 4, 2, 4)
SPLIT = ("sect", "z_lo", "x")
PAIR = [(0, 1), (1, 0)]


def spread(values, axes):
    count = lax.axis_size(axes)
    return lax.all_to_all(
        jnp.broadcast_to(values[None], (count,) + values.shape), axes, 0, 0, tiled=True
    )


def combine(every):
    student_max = jnp.max(every[:, 0], axis=0)
    teacher_max = jnp.max(every[:, 1], axis=0)
    lower = every[:, 0] - student_max
    scale = jnp.exp(lower)
    return jnp.stack(
        [
            student_max,
            teacher_max,
            jnp.sum(every[:, 2] * scale, axis=0),
            jnp.sum((every[:, 3] + every[:, 2] * lower) * scale, axis=0),
            jnp.sum(every[:, 4] * scale, axis=0),
            jnp.sum(every[:, 5] * jnp.exp(every[:, 1] - teacher_max), axis=0),
            jnp.sum(every[:, 6], axis=0),
            jnp.zeros_like(student_max),
        ]
    )


def body(hidden, head_weight, teacher_logits, sampled_ids, behaviour_logprob, valid_mask):
    width_part, col_count = head_weight.shape
    sect, z_lo, x_at, z_hi, y_at = (lax.axis_index(name) for name in AXES)
    quarter = col_count // 4
    half = 4 * width_part
    f32, bf16 = jnp.float32, jnp.bfloat16

    weight_parts = head_weight.reshape(width_part, 4, quarter).transpose(1, 0, 2)
    weight_half = lax.all_to_all(weight_parts, "y", 0, 0, tiled=True).reshape(half, quarter)

    piece = lax.dynamic_slice_in_dim(hidden, 64 * sect + 16 * x_at, 16, axis=0)
    far_piece = lax.ppermute(
        lax.dynamic_slice_in_dim(piece, half * (1 - z_hi), half, axis=1), "z_hi", PAIR
    )
    near_piece = lax.dynamic_slice_in_dim(piece, half * z_hi, half, axis=1)

    def all_pieces(values):
        return spread(spread(spread(values, "y"), "x"), "sect").reshape(512, half)

    far_rows = all_pieces(far_piece)
    far_logits = lax.ppermute(
        jnp.dot(far_rows, weight_half, preferred_element_type=f32), "z_hi", PAIR
    )
    near_rows = all_pieces(near_piece)
    logits = jnp.dot(near_rows, weight_half, preferred_element_type=f32) + far_logits

    teacher = lax.all_to_all(
        teacher_logits.reshape(64, 8, quarter).transpose(1, 0, 2), ("sect", "y"), 0, 0, tiled=True
    )
    teacher = (
        teacher.reshape(2, 4, 4, 16, quarter).transpose(0, 2, 1, 3, 4).reshape(512, quarter)
    ).astype(f32)

    rows = lax.all_gather(
        jnp.stack([sampled_ids.astype(f32), behaviour_logprob, valid_mask.astype(f32)]),
        ("z_hi", "y"),
    )
    valid_count = jnp.sum(rows[:, 2])
    rows = lax.dynamic_slice_in_dim(rows, 4 * z_hi, 4, axis=0)
    rows = rows.reshape(4, 3, 2, 4, 16).transpose(1, 2, 3, 0, 4).reshape(3, 512)
    ids, behaviour, valid = rows[0].astype(jnp.int32), rows[1], rows[2]

    first_col = (((z_lo * 4 + x_at) * 2 + sect) * 4 + y_at) * quarter
    matches = lax.broadcasted_iota(jnp.int32, logits.shape, 1) == (ids - first_col)[:, None]
    own_max = jnp.max(logits, axis=1)
    own_teacher_max = jnp.max(teacher, axis=1)
    own_shifted = logits - own_max[:, None]
    own_powers = jnp.exp(own_shifted)
    own = jnp.stack(
        [
            own_max,
            own_teacher_max,
            jnp.sum(own_powers, axis=1),
            jnp.sum(own_powers * own_shifted, axis=1),
            jnp.sum(own_powers * teacher, axis=1),
            jnp.sum(jnp.exp(teacher - own_teacher_max[:, None]), axis=1),
            jnp.sum(jnp.where(matches, logits, 0.0), axis=1),
            jnp.zeros_like(own_max),
        ]
    )
    for axes in STAGES:
        own = combine(spread(own, axes))
    student_max, teacher_max, student_sum, shifted_sum, teacher_mix, teacher_sum, sampled_logit = (
        own[i] for i in range(7)
    )
    log_student = jnp.log(student_sum)
    student_lse = student_max + log_student
    teacher_lse = teacher_max + jnp.log(teacher_sum)
    entropy = log_student - shifted_sum / student_sum
    token_kl = shifted_sum / student_sum - log_student - teacher_mix / student_sum + teacher_lse
    ratio_weight = jnp.minimum(jnp.exp(sampled_logit - student_lse - behaviour), CLIP_RATIO)
    row_factor = valid * ratio_weight / valid_count
    near_grad = (
        row_factor[:, None]
        * (jnp.exp(logits - student_max[:, None]) / student_sum[:, None])
        * (logits - student_lse[:, None] - (teacher - teacher_lse[:, None]) - token_kl[:, None])
    ).astype(bf16)

    def own_rows(values):
        kept = values.reshape((2, 4, 4, 16) + values.shape[1:])
        return lax.dynamic_index_in_dim(kept, y_at, axis=2, keepdims=False).reshape(
            (128,) + values.shape[1:]
        )

    near_all = spread(near_grad, "y")
    far_all = spread(lax.ppermute(near_grad, "z_hi", PAIR), "y")
    logit_grad = lax.dynamic_index_in_dim(
        near_all.reshape(4, 2, 4, 4, 16, quarter), y_at, axis=3, keepdims=False
    )
    logit_grad = logit_grad.transpose(1, 2, 3, 0, 4).reshape(128, col_count)

    def parts_of(grads):
        return lax.dot_general(
            grads, weight_parts, (((0, 2), (0, 2)), ((), ())), preferred_element_type=f32
        )

    near_part, far_part = parts_of(near_all), parts_of(far_all)
    both = jnp.stack([near_part, far_part])
    both = jnp.where(z_hi == 0, both, both[::-1]).reshape(2, 2, 4, 4, 4, 4, width_part)
    both = both.transpose(1, 4, 2, 0, 3, 5, 6).reshape(32, 32, width_part)
    summed = jnp.sum(
        lax.all_to_all(both, SPLIT, 0, 0, tiled=True).reshape(32, 32, width_part), axis=0
    ).astype(bf16)
    hidden_grad = lax.all_to_all(
        jnp.broadcast_to(summed.reshape(1, 8, 4, width_part), (32, 8, 4, width_part)).reshape(
            256, 4, width_part
        ),
        AXES,
        0,
        0,
        tiled=True,
    )
    hidden_grad = (
        hidden_grad.reshape(2, 4, 4, 8, 4, width_part)
        .transpose(0, 2, 1, 4, 3, 5)
        .reshape(128, 8 * width_part)
    )

    def weight_part(rows_in, grads):
        held = lax.dynamic_slice_in_dim(rows_in, width_part * y_at, width_part, axis=1)
        return lax.dot_general(
            held, grads, (((0,), (1,)), ((), ())), preferred_element_type=f32
        )

    weight_grad = (weight_part(near_rows, near_all) + weight_part(far_rows, far_all)).astype(bf16)
    return (
        logit_grad,
        hidden_grad,
        weight_grad.reshape(width_part, col_count),
        own_rows(entropy),
        own_rows(token_kl),
    )


STAGES = (SPLIT, "y")


def solution(mesh):
    wide = Mesh(mesh.devices.reshape(SIZES), AXES)
    seq, vocab = ("z_hi", "y"), ("z_lo", "x")
    by_cols = P(seq, vocab + ("sect",))
    by_row = P(seq)
    return jax.shard_map(
        body,
        mesh=wide,
        in_specs=(P(seq, None), by_cols, P(seq + ("sect",), vocab), by_row, by_row, by_row),
        out_specs=(by_cols, P(seq, None), by_cols, by_row, by_row),
        check_vma=False,
    )
```

```python
import jax
import jax.numpy as jnp
from jax import lax
from jax.sharding import Mesh, PartitionSpec as P

CLIP_RATIO = 2.0
AXES = ("sect", "z_lo", "x", "z_hi", "y")
SIZES = (2, 4, 4, 2, 4)
SPLIT = ("sect", "z_lo", "x")
PAIR = [(0, 1), (1, 0)]


def spread(values, axes):
    count = lax.axis_size(axes)
    return lax.all_to_all(
        jnp.broadcast_to(values[None], (count,) + values.shape), axes, 0, 0, tiled=True
    )


def shift(values, axis, step):
    count = lax.axis_size(axis)
    return lax.ppermute(values, axis, [(i, (i + step) % count) for i in range(count)])


def in_order(first, later, at):
    count = len(later) + 1
    held = jnp.zeros((count,) + first.shape, first.dtype)
    for step, part in enumerate([first] + later):
        held = lax.dynamic_update_index_in_dim(held, part, lax.rem(at + count - step, count), 0)
    return held


def combine(every):
    student_max = jnp.max(every[:, 0], axis=0)
    teacher_max = jnp.max(every[:, 1], axis=0)
    lower = every[:, 0] - student_max
    scale = jnp.exp(lower)
    return jnp.stack(
        [
            student_max,
            teacher_max,
            jnp.sum(every[:, 2] * scale, axis=0),
            jnp.sum((every[:, 3] + every[:, 2] * lower) * scale, axis=0),
            jnp.sum(every[:, 4] * scale, axis=0),
            jnp.sum(every[:, 5] * jnp.exp(every[:, 1] - teacher_max), axis=0),
            jnp.sum(every[:, 6], axis=0),
            jnp.zeros_like(student_max),
        ]
    )


def body(hidden, head_weight, teacher_logits, sampled_ids, behaviour_logprob, valid_mask):
    width_part, col_count = head_weight.shape
    sect, z_lo, x_at, z_hi, y_at = (lax.axis_index(name) for name in AXES)
    quarter = col_count // 4
    half = 4 * width_part
    f32, bf16 = jnp.float32, jnp.bfloat16

    weight_parts = head_weight.reshape(width_part, 4, quarter).transpose(1, 0, 2)

    def weight_for(step):
        return lax.dynamic_index_in_dim(weight_parts, lax.rem(y_at + step, 4), 0, keepdims=False)

    weight_half = in_order(
        weight_for(0), [shift(weight_for(step), "y", step) for step in (1, 2, 3)], y_at
    ).reshape(half, quarter)

    piece = lax.dynamic_slice_in_dim(hidden, 64 * sect + 16 * x_at, 16, axis=0)
    far_piece = lax.ppermute(
        lax.dynamic_slice_in_dim(piece, half * (1 - z_hi), half, axis=1), "z_hi", PAIR
    )
    near_piece = lax.dynamic_slice_in_dim(piece, half * z_hi, half, axis=1)

    def all_pieces(values):
        return spread(spread(spread(values, "y"), "x"), "sect").reshape(512, half)

    far_rows = all_pieces(far_piece)
    far_logits = lax.ppermute(
        jnp.dot(far_rows, weight_half, preferred_element_type=f32), "z_hi", PAIR
    )
    near_rows = all_pieces(near_piece)
    logits = jnp.dot(near_rows, weight_half, preferred_element_type=f32) + far_logits

    teacher = lax.all_to_all(
        teacher_logits.reshape(64, 8, quarter).transpose(1, 0, 2), ("sect", "y"), 0, 0, tiled=True
    )
    teacher = (
        teacher.reshape(2, 4, 4, 16, quarter).transpose(0, 2, 1, 3, 4).reshape(512, quarter)
    ).astype(f32)

    rows = jnp.stack(
        [sampled_ids.astype(f32), behaviour_logprob, valid_mask.astype(f32)]
        + [jnp.zeros_like(behaviour_logprob)] * 5
    )
    rows = spread(rows, "y")
    near_count = jnp.sum(rows[:, 2])
    valid_count = near_count + lax.ppermute(
        jnp.broadcast_to(near_count, (8, 128)), "z_hi", PAIR
    )[0, 0]
    rows = rows[:, :3].reshape(4, 3, 2, 4, 16).transpose(1, 2, 3, 0, 4).reshape(3, 512)
    ids, behaviour, valid = rows[0].astype(jnp.int32), rows[1], rows[2]

    first_col = (((z_lo * 4 + x_at) * 2 + sect) * 4 + y_at) * quarter
    matches = lax.broadcasted_iota(jnp.int32, logits.shape, 1) == (ids - first_col)[:, None]
    own_max = jnp.max(logits, axis=1)
    own_teacher_max = jnp.max(teacher, axis=1)
    own_shifted = logits - own_max[:, None]
    own_powers = jnp.exp(own_shifted)
    own = jnp.stack(
        [
            own_max,
            own_teacher_max,
            jnp.sum(own_powers, axis=1),
            jnp.sum(own_powers * own_shifted, axis=1),
            jnp.sum(own_powers * teacher, axis=1),
            jnp.sum(jnp.exp(teacher - own_teacher_max[:, None]), axis=1),
            jnp.sum(jnp.where(matches, logits, 0.0), axis=1),
            jnp.zeros_like(own_max),
        ]
    )
    for axes in STAGES:
        own = combine(spread(own, axes))
    student_max, teacher_max, student_sum, shifted_sum, teacher_mix, teacher_sum, sampled_logit = (
        own[i] for i in range(7)
    )
    log_student = jnp.log(student_sum)
    student_lse = student_max + log_student
    teacher_lse = teacher_max + jnp.log(teacher_sum)
    entropy = log_student - shifted_sum / student_sum
    token_kl = shifted_sum / student_sum - log_student - teacher_mix / student_sum + teacher_lse
    ratio_weight = jnp.minimum(jnp.exp(sampled_logit - student_lse - behaviour), CLIP_RATIO)
    row_factor = valid * ratio_weight / valid_count
    near_grad = (
        row_factor[:, None]
        * (jnp.exp(logits - student_max[:, None]) / student_sum[:, None])
        * (logits - student_lse[:, None] - (teacher - teacher_lse[:, None]) - token_kl[:, None])
    ).astype(bf16)

    def own_rows(values):
        kept = values.reshape((2, 4, 4, 16) + values.shape[1:])
        return lax.dynamic_index_in_dim(kept, y_at, axis=2, keepdims=False).reshape(
            (128,) + values.shape[1:]
        )

    near_all = spread(near_grad, "y")
    far_grad = lax.ppermute(near_grad, "z_hi", PAIR)
    far_all = in_order(far_grad, [shift(far_grad, "y", step) for step in (1, 2, 3)], y_at)
    logit_grad = lax.dynamic_index_in_dim(
        near_all.reshape(4, 2, 4, 4, 16, quarter), y_at, axis=3, keepdims=False
    )
    logit_grad = logit_grad.transpose(1, 2, 3, 0, 4).reshape(128, col_count)

    def summed(grads):
        part = lax.dot_general(
            grads, weight_parts, (((0, 2), (0, 2)), ((), ())), preferred_element_type=f32
        ).reshape(2, 256, width_part)
        kept = lax.dynamic_index_in_dim(part, sect, 0, keepdims=False)
        given = lax.dynamic_index_in_dim(part, 1 - sect, 0, keepdims=False)
        kept = kept + lax.ppermute(given, "sect", PAIR)
        kept = kept.reshape(4, 4, 4, 4, width_part).transpose(2, 0, 1, 3, 4)
        kept = lax.all_to_all(kept.reshape(16, 16, width_part), ("z_lo", "x"), 0, 0, tiled=True)
        return jnp.sum(kept, axis=0).astype(bf16)

    near_sum, far_sum = summed(near_all), summed(far_all)
    both = jnp.where(
        z_hi == 0, jnp.stack([near_sum, far_sum]), jnp.stack([far_sum, near_sum])
    )
    mine = lax.all_to_all(
        jnp.broadcast_to(both.reshape(1, 8, 4, width_part), (16, 8, 4, width_part)).reshape(
            128, 4, width_part
        ),
        AXES[1:],
        0,
        0,
        tiled=True,
    )
    mine = (
        mine.reshape(4, 4, 8, 4, width_part)
        .transpose(1, 0, 3, 2, 4)
        .reshape(64, 8 * width_part)
    )
    other = lax.ppermute(mine, "sect", PAIR)
    hidden_grad = jnp.where(
        sect == 0, jnp.concatenate([mine, other]), jnp.concatenate([other, mine])
    )

    def weight_part(rows_in, grads):
        held = lax.dynamic_slice_in_dim(rows_in, width_part * y_at, width_part, axis=1)
        return lax.dot_general(
            held, grads, (((0,), (1,)), ((), ())), preferred_element_type=f32
        )

    weight_grad = (weight_part(near_rows, near_all) + weight_part(far_rows, far_all)).astype(bf16)
    return (
        logit_grad,
        hidden_grad,
        weight_grad.reshape(width_part, col_count),
        own_rows(entropy),
        own_rows(token_kl),
    )


STAGES = (("sect", "x"), ("z_lo", "y"))


def solution(mesh):
    wide = Mesh(mesh.devices.reshape(SIZES), AXES)
    seq, vocab = ("z_hi", "y"), ("z_lo", "x")
    by_cols = P(seq, vocab + ("sect",))
    by_row = P(seq)
    return jax.shard_map(
        body,
        mesh=wide,
        in_specs=(P(seq, None), by_cols, P(seq + ("sect",), vocab), by_row, by_row, by_row),
        out_specs=(by_cols, P(seq, None), by_cols, by_row, by_row),
        check_vma=False,
    )
```

```python
import jax
import jax.numpy as jnp
from jax import lax
from jax.sharding import Mesh, PartitionSpec as P

CLIP_RATIO = 2.0
AXES = ("sect", "z_lo", "x", "z_hi", "y")
SIZES = (2, 4, 4, 2, 4)
SPLIT = ("sect", "z_lo", "x")
PAIR = [(0, 1), (1, 0)]


def spread(values, axes):
    count = lax.axis_size(axes)
    return lax.all_to_all(
        jnp.broadcast_to(values[None], (count,) + values.shape), axes, 0, 0, tiled=True
    )


def shift(values, axis, step):
    count = lax.axis_size(axis)
    return lax.ppermute(values, axis, [(i, (i + step) % count) for i in range(count)])


def after(values, earlier):
    return values + (earlier[(0,) * earlier.ndim] * 0).astype(values.dtype)


def in_order(first, later, at):
    count = len(later) + 1
    held = jnp.zeros((count,) + first.shape, first.dtype)
    for step, part in enumerate([first] + later):
        held = lax.dynamic_update_index_in_dim(held, part, lax.rem(at + count - step, count), 0)
    return held


def contract_cols(left_side, right_side):
    return lax.dot_general(
        left_side, right_side, (((1,), (1,)), ((), ())), preferred_element_type=jnp.float32
    )


def contract_rows(left_side, right_side):
    return lax.dot_general(
        left_side, right_side, (((0,), (0,)), ((), ())), preferred_element_type=jnp.float32
    )


def combine(every):
    student_max = jnp.max(every[:, 0], axis=0)
    teacher_max = jnp.max(every[:, 1], axis=0)
    lower = every[:, 0] - student_max
    scale = jnp.exp(lower)
    return jnp.stack(
        [
            student_max,
            teacher_max,
            jnp.sum(every[:, 2] * scale, axis=0),
            jnp.sum((every[:, 3] + every[:, 2] * lower) * scale, axis=0),
            jnp.sum(every[:, 4] * scale, axis=0),
            jnp.sum(every[:, 5] * jnp.exp(every[:, 1] - teacher_max), axis=0),
            jnp.sum(every[:, 6], axis=0),
            jnp.zeros_like(student_max),
        ]
    )


def body(hidden, head_weight, teacher_logits, sampled_ids, behaviour_logprob, valid_mask):
    width_part, col_count = head_weight.shape
    sect, z_lo, x_at, z_hi, y_at = (lax.axis_index(name) for name in AXES)
    quarter = col_count // 4
    half = 4 * width_part
    f32, bf16 = jnp.float32, jnp.bfloat16

    piece = lax.dynamic_slice_in_dim(hidden, 64 * sect + 16 * x_at, 16, axis=0)
    far_piece = lax.ppermute(
        lax.dynamic_slice_in_dim(piece, half * (1 - z_hi), half, axis=1), "z_hi", PAIR
    )
    near_piece = lax.dynamic_slice_in_dim(piece, half * z_hi, half, axis=1)
    mask = valid_mask.astype(f32)
    far_mask = lax.ppermute(mask, "z_hi", PAIR)

    weight_parts = head_weight.T.reshape(4, quarter, width_part)

    def weight_for(step):
        return lax.dynamic_index_in_dim(weight_parts, lax.rem(y_at + step, 4), 0, keepdims=False)

    weight_half = in_order(
        weight_for(0), [shift(weight_for(step), "y", step) for step in (1, 2, 3)], y_at
    )

    def logits_of(values):
        return sum(
            contract_cols(
                lax.slice_in_dim(values, k * width_part, (k + 1) * width_part, axis=1),
                weight_half[k],
            )
            for k in range(4)
        )

    pieces = spread(jnp.stack([far_piece, near_piece]), "y")

    def all_pieces(values):
        return spread(spread(values, "x"), "sect").reshape(512, half)

    far_rows = all_pieces(pieces[:, 0])
    given_logits = logits_of(far_rows)
    far_logits = lax.ppermute(given_logits, "z_hi", PAIR)
    near_rows = all_pieces(after(pieces[:, 1], given_logits))
    logits = logits_of(near_rows) + far_logits

    teacher = lax.all_to_all(
        after(teacher_logits, given_logits).reshape(64, 8, quarter).transpose(1, 0, 2), ("sect", "y"), 0, 0, tiled=True
    )
    teacher = (
        teacher.reshape(2, 4, 4, 16, quarter).transpose(0, 2, 1, 3, 4).reshape(512, quarter)
    ).astype(f32)

    rows = jnp.stack(
        [sampled_ids.astype(f32), behaviour_logprob, mask, far_mask]
        + [jnp.zeros_like(behaviour_logprob)] * 4
    )
    rows = spread(after(rows, given_logits), "y")
    valid_count = jnp.sum(rows[:, 2:4])
    rows = rows[:, :3].reshape(4, 3, 2, 4, 16).transpose(1, 2, 3, 0, 4).reshape(3, 512)
    ids, behaviour, valid = rows[0].astype(jnp.int32), rows[1], rows[2]

    first_col = (((z_lo * 4 + x_at) * 2 + sect) * 4 + y_at) * quarter
    matches = lax.broadcasted_iota(jnp.int32, logits.shape, 1) == (ids - first_col)[:, None]
    own_max = jnp.max(logits, axis=1)
    own_teacher_max = jnp.max(teacher, axis=1)
    own_shifted = logits - own_max[:, None]
    own_powers = jnp.exp(own_shifted)
    own = jnp.stack(
        [
            own_max,
            own_teacher_max,
            jnp.sum(own_powers, axis=1),
            jnp.sum(own_powers * own_shifted, axis=1),
            jnp.sum(own_powers * teacher, axis=1),
            jnp.sum(jnp.exp(teacher - own_teacher_max[:, None]), axis=1),
            jnp.sum(jnp.where(matches, logits, 0.0), axis=1),
            jnp.zeros_like(own_max),
        ]
    )
    for axes in STAGES:
        own = combine(spread(own, axes))
    student_max, teacher_max, student_sum, shifted_sum, teacher_mix, teacher_sum, sampled_logit = (
        own[i] for i in range(7)
    )
    log_student = jnp.log(student_sum)
    student_lse = student_max + log_student
    teacher_lse = teacher_max + jnp.log(teacher_sum)
    entropy = log_student - shifted_sum / student_sum
    token_kl = shifted_sum / student_sum - log_student - teacher_mix / student_sum + teacher_lse
    ratio_weight = jnp.minimum(jnp.exp(sampled_logit - student_lse - behaviour), CLIP_RATIO)
    row_factor = valid * ratio_weight / valid_count
    near_grad = (
        row_factor[:, None]
        * (jnp.exp(logits - student_max[:, None]) / student_sum[:, None])
        * (logits - student_lse[:, None] - (teacher - teacher_lse[:, None]) - token_kl[:, None])
    ).astype(bf16)

    def own_rows(values):
        kept = values.reshape((2, 4, 4, 16) + values.shape[1:])
        return lax.dynamic_index_in_dim(kept, y_at, axis=2, keepdims=False).reshape(
            (128,) + values.shape[1:]
        )

    near_grad = near_grad.T
    near_all = spread(near_grad, "y")
    far_grad = after(lax.ppermute(near_grad, "z_hi", PAIR), near_all)
    far_all = in_order(far_grad, [shift(far_grad, "y", step) for step in (1, 2, 3)], y_at)
    logit_grad = lax.dynamic_index_in_dim(
        near_all.reshape(4, quarter, 2, 4, 4, 16), y_at, axis=4, keepdims=False
    )
    logit_grad = logit_grad.reshape(col_count, 128).T
    near_all = near_all.reshape(col_count, 512)
    far_all = far_all.reshape(col_count, 512)
    weight_cols = weight_parts.reshape(col_count, width_part)

    def summed(grads, earlier, flip):
        part = contract_rows(grads, weight_cols).reshape(2, 256, width_part)
        kept = lax.dynamic_index_in_dim(part, sect, 0, keepdims=False)
        given = lax.dynamic_index_in_dim(part, 1 - sect, 0, keepdims=False)
        if earlier is not None:
            given = after(given, earlier)
        kept = kept + lax.ppermute(given, "sect", PAIR)
        kept = kept.reshape(4, 4, 16, width_part).transpose(1, 0, 2, 3)
        kept = lax.all_to_all(kept.reshape(16, 16, width_part), ("z_lo", "x"), 0, 0, tiled=True)
        moves = [
            ((j * 2 + z) * 4 + k, (k * 2 + (z ^ flip)) * 4 + j)
            for j in range(4)
            for z in range(2)
            for k in range(4)
        ]
        kept = jnp.sum(kept, axis=0).astype(bf16)
        return lax.ppermute(kept, ("z_lo", "z_hi", "y"), moves)

    near_sum = summed(near_all, None, 0)
    far_sum = summed(far_all, near_sum, 1)
    both = jnp.where(
        z_hi == 0,
        jnp.concatenate([near_sum, far_sum], axis=1),
        jnp.concatenate([far_sum, near_sum], axis=1),
    )
    mine = spread(both, ("z_lo", "x"))
    mine = (
        mine.reshape(4, 4, 16, 2, width_part)
        .transpose(1, 2, 3, 0, 4)
        .reshape(64, 8 * width_part)
    )
    other = lax.ppermute(mine, "sect", PAIR)
    hidden_grad = jnp.where(
        sect == 0, jnp.concatenate([mine, other]), jnp.concatenate([other, mine])
    )

    def weight_part(rows_in, grads):
        held = lax.dynamic_slice_in_dim(rows_in, width_part * y_at, width_part, axis=1)
        return jnp.dot(grads, held, preferred_element_type=f32)

    weight_grad = (weight_part(near_rows, near_all) + weight_part(far_rows, far_all)).astype(bf16).T
    return (
        logit_grad,
        hidden_grad,
        weight_grad,
        own_rows(entropy),
        own_rows(token_kl),
    )


STAGES = (("sect", "x"), ("z_lo", "y"))


def solution(mesh):
    wide = Mesh(mesh.devices.reshape(SIZES), AXES)
    seq, vocab = ("z_hi", "y"), ("z_lo", "x")
    by_cols = P(seq, vocab + ("sect",))
    by_row = P(seq)
    return jax.shard_map(
        body,
        mesh=wide,
        in_specs=(P(seq, None), by_cols, P(seq + ("sect",), vocab), by_row, by_row, by_row),
        out_specs=(by_cols, P(seq, None), by_cols, by_row, by_row),
        check_vma=False,
    )
```

```python
import jax
import jax.numpy as jnp
from jax import lax
from jax.sharding import Mesh, PartitionSpec as P

CLIP_RATIO = 2.0
AXES = ("sect", "z_lo", "x", "z_hi", "y")
SIZES = (2, 4, 4, 2, 4)
SPLIT = ("sect", "z_lo", "x")
PAIR = [(0, 1), (1, 0)]


def spread(values, axes):
    count = lax.axis_size(axes)
    return lax.all_to_all(
        jnp.broadcast_to(values[None], (count,) + values.shape), axes, 0, 0, tiled=True
    )


def shift(values, axis, step):
    count = lax.axis_size(axis)
    return lax.ppermute(values, axis, [(i, (i + step) % count) for i in range(count)])


def after(values, earlier):
    return values + (earlier[(0,) * earlier.ndim] * 0).astype(values.dtype)


def in_order(first, later, at):
    count = len(later) + 1
    held = jnp.zeros((count,) + first.shape, first.dtype)
    for step, part in enumerate([first] + later):
        held = lax.dynamic_update_index_in_dim(held, part, lax.rem(at + count - step, count), 0)
    return held


def contract_cols(left_side, right_side):
    return lax.dot_general(
        left_side, right_side, (((1,), (1,)), ((), ())), preferred_element_type=jnp.float32
    )


def combine(every):
    student_max = jnp.max(every[:, 0], axis=0)
    teacher_max = jnp.max(every[:, 1], axis=0)
    lower = every[:, 0] - student_max
    scale = jnp.exp(lower)
    return jnp.stack(
        [
            student_max,
            teacher_max,
            jnp.sum(every[:, 2] * scale, axis=0),
            jnp.sum((every[:, 3] + every[:, 2] * lower) * scale, axis=0),
            jnp.sum(every[:, 4] * scale, axis=0),
            jnp.sum(every[:, 5] * jnp.exp(every[:, 1] - teacher_max), axis=0),
            jnp.sum(every[:, 6], axis=0),
            jnp.zeros_like(student_max),
        ]
    )


def body(hidden, head_weight, teacher_logits, sampled_ids, behaviour_logprob, valid_mask):
    width_part, col_count = head_weight.shape
    sect, z_lo, x_at, z_hi, y_at = (lax.axis_index(name) for name in AXES)
    quarter = col_count // 4
    half = 4 * width_part
    f32, bf16 = jnp.float32, jnp.bfloat16

    piece = lax.dynamic_slice_in_dim(hidden, 64 * sect + 16 * x_at, 16, axis=0)
    far_piece = lax.ppermute(
        lax.dynamic_slice_in_dim(piece, half * (1 - z_hi), half, axis=1), "z_hi", PAIR
    )
    near_piece = lax.dynamic_slice_in_dim(piece, half * z_hi, half, axis=1)

    weight_parts = head_weight.T.reshape(4, quarter, width_part)

    def weight_for(step):
        return lax.dynamic_index_in_dim(weight_parts, lax.rem(y_at + step, 4), 0, keepdims=False)

    weight_half = in_order(
        weight_for(0), [shift(weight_for(step), "y", step) for step in (1, 2, 3)], y_at
    )

    def logits_of(values):
        return sum(
            contract_cols(
                weight_half[k],
                lax.slice_in_dim(values, k * width_part, (k + 1) * width_part, axis=1),
            )
            for k in range(4)
        )

    def turned(values, axis):
        first, second = jnp.split(values, 2, axis=axis)
        return jnp.where(sect == 0, values, jnp.concatenate([second, first], axis=axis))

    pieces = spread(spread(jnp.stack([far_piece, near_piece]), "y"), "x")
    other_pieces = lax.ppermute(pieces, "sect", PAIR)
    far_halves = [kept[:, :, 0].reshape(256, half) for kept in (pieces, other_pieces)]
    near_halves = [kept[:, :, 1].reshape(256, half) for kept in (pieces, other_pieces)]
    given_logits = [logits_of(values) for values in far_halves]
    far_logits = [lax.ppermute(values, "z_hi", PAIR) for values in given_logits]
    far_rows = jnp.concatenate(far_halves)
    near_rows = jnp.concatenate(near_halves)
    logits = jnp.concatenate(
        [
            logits_of(near_halves[0]) + after(far_logits[0], given_logits[1]),
            logits_of(near_halves[1]) + far_logits[1],
        ],
        axis=1,
    )

    teacher = lax.all_to_all(
        teacher_logits.reshape(64, 8, quarter).transpose(1, 0, 2), ("sect", "y"), 0, 0, tiled=True
    )
    teacher = teacher.reshape(2, 4, 4, 16, quarter)
    teacher = jnp.stack(
        [lax.dynamic_index_in_dim(teacher, at, 0, keepdims=False) for at in (sect, 1 - sect)]
    )
    teacher = teacher.transpose(0, 2, 1, 3, 4).reshape(512, quarter).T.astype(f32)

    rows = jnp.stack(
        [sampled_ids.astype(f32), behaviour_logprob, valid_mask.astype(f32)]
        + [jnp.zeros_like(behaviour_logprob)] * 5
    )
    rows = spread(after(rows, given_logits[1]), "y")
    near_count = jnp.sum(rows[:, 2])
    valid_count = near_count + lax.ppermute(
        jnp.broadcast_to(near_count, (8, 128)), "z_hi", PAIR
    )[0, 0]
    rows = rows[:, :3].reshape(4, 3, 2, 4, 16).transpose(1, 2, 3, 0, 4)
    rows = turned(rows, 1).reshape(3, 512)
    ids, behaviour, valid = rows[0].astype(jnp.int32), rows[1], rows[2]

    first_col = (((z_lo * 4 + x_at) * 2 + sect) * 4 + y_at) * quarter
    matches = lax.broadcasted_iota(jnp.int32, logits.shape, 0) == ids - first_col
    own_max = jnp.max(logits, axis=0)
    own_teacher_max = jnp.max(teacher, axis=0)
    own_shifted = logits - own_max
    own_powers = jnp.exp(own_shifted)
    own = jnp.stack(
        [
            own_max,
            own_teacher_max,
            jnp.sum(own_powers, axis=0),
            jnp.sum(own_powers * own_shifted, axis=0),
            jnp.sum(own_powers * teacher, axis=0),
            jnp.sum(jnp.exp(teacher - own_teacher_max), axis=0),
            jnp.sum(jnp.where(matches, logits, 0.0), axis=0),
            jnp.zeros_like(own_max),
        ]
    )
    own = turned(after(own, valid_count), 1)
    for axes in STAGES:
        own = combine(spread(own, axes))
    own = turned(own, 1)
    student_max, teacher_max, student_sum, shifted_sum, teacher_mix, teacher_sum, sampled_logit = (
        own[i] for i in range(7)
    )
    log_student = jnp.log(student_sum)
    student_lse = student_max + log_student
    teacher_lse = teacher_max + jnp.log(teacher_sum)
    entropy = log_student - shifted_sum / student_sum
    token_kl = shifted_sum / student_sum - log_student - teacher_mix / student_sum + teacher_lse
    ratio_weight = jnp.minimum(jnp.exp(sampled_logit - student_lse - behaviour), CLIP_RATIO)
    row_factor = valid * ratio_weight / valid_count
    near_grad = (
        row_factor
        * (jnp.exp(logits - student_max) / student_sum)
        * (logits - student_lse - (teacher - teacher_lse) - token_kl)
    ).astype(bf16)

    def own_rows(values):
        kept = turned(values.reshape(2, 4, 4, 16), 0)
        return lax.dynamic_index_in_dim(kept, y_at, axis=2, keepdims=False).reshape(128)

    def ring(values):
        cut = quarter // 2
        back, ahead = shift(values, "y", 1), shift(values, "y", 3)
        opposite = jnp.concatenate([shift(back[:cut], "y", 1), shift(ahead[cut:], "y", 3)])
        return in_order(values, [back, opposite, ahead], y_at)

    near_all = ring(near_grad)
    far_all = ring(lax.ppermute(near_grad, "z_hi", PAIR))
    logit_grad = lax.dynamic_index_in_dim(
        near_all.reshape(4, quarter, 2, 4, 4, 16), y_at, axis=4, keepdims=False
    )
    logit_grad = turned(logit_grad, 2).reshape(col_count, 128).T

    def sect_sum(grads):
        part = lax.dot_general(
            grads.reshape(col_count, 512),
            weight_parts.reshape(col_count, width_part),
            (((0,), (0,)), ((), ())),
            preferred_element_type=f32,
        )
        return part[:256] + lax.ppermute(part[256:], "sect", PAIR)

    def split_sum(kept):
        kept = kept.reshape(2, 4, 4, 16, width_part).transpose(2, 1, 0, 3, 4)
        kept = lax.all_to_all(kept.reshape(16, 32, width_part), ("z_lo", "x"), 0, 0, tiled=True)
        return jnp.sum(kept, axis=0).astype(bf16)

    def handed_over(kept, flip):
        moves = [
            ((j * 2 + z) * 4 + k, (k * 2 + (z ^ flip)) * 4 + j)
            for j in range(4)
            for z in range(2)
            for k in range(4)
        ]
        return lax.ppermute(kept, ("z_lo", "z_hi", "y"), moves)

    def weight_part(rows_in, grads, earlier):
        held = lax.dynamic_slice_in_dim(rows_in, width_part * y_at, width_part, axis=1)
        return jnp.dot(
            grads.reshape(col_count, 512), after(held, earlier), preferred_element_type=f32
        )

    near_kept = sect_sum(near_all)
    far_kept = sect_sum(far_all)
    sums = split_sum(jnp.stack([near_kept, far_kept]))
    weight_grad = (
        (weight_part(near_rows, near_all, near_kept) + weight_part(far_rows, far_all, far_kept))
        .astype(bf16)
        .T
    )
    sums = after(after(sums, weight_grad), logit_grad)
    near_sum, far_sum = handed_over(sums[:16], 0), handed_over(sums[16:], 1)
    both = jnp.where(
        z_hi == 0,
        jnp.concatenate([near_sum, far_sum], axis=1),
        jnp.concatenate([far_sum, near_sum], axis=1),
    )
    mine = spread(both, ("z_lo", "x"))
    mine = (
        mine.reshape(4, 4, 16, 2, width_part)
        .transpose(1, 2, 3, 0, 4)
        .reshape(64, 8 * width_part)
    )
    other = lax.ppermute(mine, "sect", PAIR)
    hidden_grad = jnp.where(
        sect == 0, jnp.concatenate([mine, other]), jnp.concatenate([other, mine])
    )

    return (
        logit_grad,
        hidden_grad,
        weight_grad,
        own_rows(entropy),
        own_rows(token_kl),
    )


STAGES = (("sect", "x"), ("z_lo", "y"))


def solution(mesh):
    wide = Mesh(mesh.devices.reshape(SIZES), AXES)
    seq, vocab = ("z_hi", "y"), ("z_lo", "x")
    by_cols = P(seq, vocab + ("sect",))
    by_row = P(seq)
    return jax.shard_map(
        body,
        mesh=wide,
        in_specs=(P(seq, None), by_cols, P(seq + ("sect",), vocab), by_row, by_row, by_row),
        out_specs=(by_cols, P(seq, None), by_cols, by_row, by_row),
        check_vma=False,
    )
```

```python
import jax
import jax.numpy as jnp
from jax import lax
from jax.sharding import Mesh, PartitionSpec as P

CLIP_RATIO = 2.0
AXES = ("sect", "z_lo", "x", "z_hi", "y")
SIZES = (2, 4, 4, 2, 4)
SPLIT = ("sect", "z_lo", "x")
PAIR = [(0, 1), (1, 0)]


def spread(values, axes):
    count = lax.axis_size(axes)
    return lax.all_to_all(
        jnp.broadcast_to(values[None], (count,) + values.shape), axes, 0, 0, tiled=True
    )


def shift(values, axis, step):
    count = lax.axis_size(axis)
    return lax.ppermute(values, axis, [(i, (i + step) % count) for i in range(count)])


def after(values, earlier):
    return values + (earlier[(0,) * earlier.ndim] * 0).astype(values.dtype)


def in_order(first, later, at):
    count = len(later) + 1
    held = jnp.zeros((count,) + first.shape, first.dtype)
    for step, part in enumerate([first] + later):
        held = lax.dynamic_update_index_in_dim(held, part, lax.rem(at + count - step, count), 0)
    return held


def contract_cols(left_side, right_side):
    return lax.dot_general(
        left_side, right_side, (((1,), (1,)), ((), ())), preferred_element_type=jnp.float32
    )


def combine(every):
    student_max = jnp.max(every[:, 0], axis=0)
    teacher_max = jnp.max(every[:, 1], axis=0)
    lower = every[:, 0] - student_max
    scale = jnp.exp(lower)
    return jnp.stack(
        [
            student_max,
            teacher_max,
            jnp.sum(every[:, 2] * scale, axis=0),
            jnp.sum((every[:, 3] + every[:, 2] * lower) * scale, axis=0),
            jnp.sum(every[:, 4] * scale, axis=0),
            jnp.sum(every[:, 5] * jnp.exp(every[:, 1] - teacher_max), axis=0),
            jnp.sum(every[:, 6], axis=0),
            jnp.zeros_like(student_max),
        ]
    )


def body(hidden, head_weight, teacher_logits, sampled_ids, behaviour_logprob, valid_mask):
    width_part, col_count = head_weight.shape
    sect, z_lo, x_at, z_hi, y_at = (lax.axis_index(name) for name in AXES)
    quarter = col_count // 4
    half = 4 * width_part
    f32, bf16 = jnp.float32, jnp.bfloat16

    piece = lax.dynamic_slice_in_dim(hidden, 64 * sect + 16 * x_at, 16, axis=0)
    far_piece = lax.ppermute(
        lax.dynamic_slice_in_dim(piece, half * (1 - z_hi), half, axis=1), "z_hi", PAIR
    )
    near_piece = lax.dynamic_slice_in_dim(piece, half * z_hi, half, axis=1)

    weight_parts = head_weight.T.reshape(4, quarter, width_part)

    def weight_for(step):
        return lax.dynamic_index_in_dim(weight_parts, lax.rem(y_at + step, 4), 0, keepdims=False)

    arrived = [shift(weight_for(step), "y", step) for step in (1, 2, 3)]
    weight_half = in_order(weight_for(0), arrived, y_at)

    def logits_of(values):
        return sum(
            contract_cols(
                weight_half[k],
                lax.slice_in_dim(values, k * width_part, (k + 1) * width_part, axis=1),
            )
            for k in range(4)
        )

    def turned(values, axis):
        first, second = jnp.split(values, 2, axis=axis)
        return jnp.where(sect == 0, values, jnp.concatenate([second, first], axis=axis))

    first_pieces = spread(jnp.stack([far_piece, near_piece]), "y")
    pieces = spread(after(after(first_pieces, arrived[0]), arrived[2]), "x")
    other_pieces = lax.ppermute(after(pieces, arrived[1]), "sect", PAIR)
    far_halves = [kept[:, :, 0].reshape(256, half) for kept in (pieces, other_pieces)]
    near_halves = [kept[:, :, 1].reshape(256, half) for kept in (pieces, other_pieces)]
    given_logits = [logits_of(values) for values in far_halves]
    far_logits = [lax.ppermute(values, "z_hi", PAIR) for values in given_logits]
    far_rows = jnp.concatenate(far_halves)
    near_rows = jnp.concatenate(near_halves)
    by_core = after(teacher_logits, given_logits[1]).reshape(64, 2, 4, quarter).transpose(1, 2, 0, 3)
    teacher_parts = jnp.stack(
        [
            lax.dynamic_index_in_dim(by_core, sect, 0, keepdims=False),
            lax.ppermute(
                lax.dynamic_index_in_dim(by_core, 1 - sect, 0, keepdims=False), "sect", PAIR
            ),
        ],
        axis=1,
    )

    def teacher_for(step):
        return lax.dynamic_index_in_dim(teacher_parts, lax.rem(y_at + step, 4), 0, keepdims=False)

    teacher = in_order(
        teacher_for(0), [shift(teacher_for(step), "y", step) for step in (1, 2, 3)], y_at
    )
    teacher = teacher.reshape(4, 2, 4, 16, quarter).transpose(1, 2, 0, 3, 4)
    teacher = teacher.reshape(512, quarter).T.astype(f32)

    logits = jnp.concatenate(
        [
            logits_of(near_halves[0]) + after(far_logits[0], teacher),
            logits_of(near_halves[1]) + far_logits[1],
        ],
        axis=1,
    )

    rows = jnp.stack(
        [sampled_ids.astype(f32), behaviour_logprob, valid_mask.astype(f32)]
        + [jnp.zeros_like(behaviour_logprob)] * 5
    )
    rows = after(rows, given_logits[1])
    rows = in_order(rows, [shift(rows, "y", step) for step in (1, 2, 3)], y_at)
    near_count = jnp.sum(rows[:, 2])
    valid_count = near_count + lax.ppermute(
        jnp.broadcast_to(near_count, (8, 128)), "z_hi", PAIR
    )[0, 0]
    rows = rows[:, :3].reshape(4, 3, 2, 4, 16).transpose(1, 2, 3, 0, 4)
    rows = turned(rows, 1).reshape(3, 512)
    ids, behaviour, valid = rows[0].astype(jnp.int32), rows[1], rows[2]

    first_col = (((z_lo * 4 + x_at) * 2 + sect) * 4 + y_at) * quarter
    matches = lax.broadcasted_iota(jnp.int32, logits.shape, 0) == ids - first_col
    own_max = jnp.max(logits, axis=0)
    own_teacher_max = jnp.max(teacher, axis=0)
    own_shifted = logits - own_max
    own_powers = jnp.exp(own_shifted)
    own = jnp.stack(
        [
            own_max,
            own_teacher_max,
            jnp.sum(own_powers, axis=0),
            jnp.sum(own_powers * own_shifted, axis=0),
            jnp.sum(own_powers * teacher, axis=0),
            jnp.sum(jnp.exp(teacher - own_teacher_max), axis=0),
            jnp.sum(jnp.where(matches, logits, 0.0), axis=0),
            jnp.zeros_like(own_max),
        ]
    )
    own = turned(after(own, valid_count), 1)
    for axes in STAGES:
        own = combine(spread(own, axes))
    own = turned(own, 1)
    student_max, teacher_max, student_sum, shifted_sum, teacher_mix, teacher_sum, sampled_logit = (
        own[i] for i in range(7)
    )
    log_student = jnp.log(student_sum)
    student_lse = student_max + log_student
    teacher_lse = teacher_max + jnp.log(teacher_sum)
    entropy = log_student - shifted_sum / student_sum
    token_kl = shifted_sum / student_sum - log_student - teacher_mix / student_sum + teacher_lse
    ratio_weight = jnp.minimum(jnp.exp(sampled_logit - student_lse - behaviour), CLIP_RATIO)
    row_factor = valid * ratio_weight / valid_count
    near_grad = (
        row_factor
        * (jnp.exp(logits - student_max) / student_sum)
        * (logits - student_lse - (teacher - teacher_lse) - token_kl)
    ).astype(bf16)

    def own_rows(values):
        kept = turned(values.reshape(2, 4, 4, 16), 0)
        return lax.dynamic_index_in_dim(kept, y_at, axis=2, keepdims=False).reshape(128)

    weight_rows = head_weight.reshape(width_part, 4, quarter).transpose(1, 0, 2)
    cut = quarter // 2

    def product(step, grads, start=0):
        held = lax.dynamic_index_in_dim(
            weight_rows, lax.rem(y_at + step, 4), 0, keepdims=False
        )[:, start : start + grads.shape[0]]
        return jnp.dot(held, grads, preferred_element_type=f32)

    def ring(values, ready=None):
        back, ahead = shift(values, "y", 1), shift(values, "y", 3)
        part = product(0, values) + product(3, back) + product(1, ahead)
        sent = (back[:cut], ahead[cut:])
        if ready is not None:
            sent = tuple(after(half_block, ready) for half_block in sent)
        top, bottom = shift(sent[0], "y", 1), shift(sent[1], "y", 3)
        opposite = jnp.concatenate([top, bottom])
        return in_order(values, [back, opposite, ahead], y_at), opposite, part

    def sect_sum(part):
        return part[:, :256] + lax.ppermute(part[:, 256:], "sect", PAIR)

    def split_sum(kept, beside, flip):
        kept = kept.T.reshape(4, 4, 16, width_part).transpose(1, 0, 2, 3)
        kept = lax.all_to_all(kept.reshape(16, 16, width_part), ("z_lo", "x"), 0, 0, tiled=True)
        kept = jnp.sum(kept, axis=0).astype(bf16)
        for values in beside:
            kept = after(kept, values)
        moves = [
            ((j * 2 + z) * 4 + k, (k * 2 + (z ^ flip)) * 4 + j)
            for j in range(4)
            for z in range(2)
            for k in range(4)
        ]
        return lax.ppermute(kept, ("z_lo", "z_hi", "y"), moves)

    def weight_part(rows_in, grads, earlier):
        held = lax.dynamic_slice_in_dim(rows_in, width_part * y_at, width_part, axis=1)
        return jnp.dot(
            grads.reshape(col_count, 512), after(held, earlier), preferred_element_type=f32
        )

    far_grad = lax.ppermute(near_grad, "z_hi", PAIR)
    near_all, near_last, near_part = ring(near_grad)
    near_kept = sect_sum(near_part + product(2, near_last))
    far_all, far_last, far_part = ring(after(far_grad, near_last), near_kept)
    near_sum = split_sum(near_kept, (), 0)
    far_kept = sect_sum(after(far_part, near_sum) + product(2, far_last))
    token = lax.broadcasted_iota(jnp.int32, (128, 512), 0)
    place = ((token // 64 ^ sect) * 4 + token // 16 % 4) * 64 + y_at * 16 + token % 16
    chosen = (place == lax.broadcasted_iota(jnp.int32, (128, 512), 1)).astype(bf16)
    logit_grad = contract_cols(chosen, near_all.reshape(col_count, 512)).astype(bf16)
    weight_grad = (
        (weight_part(near_rows, near_all, near_kept) + weight_part(far_rows, far_all, far_kept))
        .astype(bf16)
        .T
    )
    far_sum = split_sum(far_kept, (weight_grad, logit_grad), 1)
    both = jnp.where(
        z_hi == 0,
        jnp.concatenate([near_sum, far_sum], axis=1),
        jnp.concatenate([far_sum, near_sum], axis=1),
    )
    mine = spread(both, ("z_lo", "x"))
    mine = (
        mine.reshape(4, 4, 16, 2, width_part)
        .transpose(1, 2, 3, 0, 4)
        .reshape(64, 8 * width_part)
    )
    other = lax.ppermute(mine, "sect", PAIR)
    hidden_grad = jnp.where(
        sect == 0, jnp.concatenate([mine, other]), jnp.concatenate([other, mine])
    )

    return (
        logit_grad,
        hidden_grad,
        weight_grad,
        own_rows(entropy),
        own_rows(token_kl),
    )


STAGES = (("sect", "x"), ("z_lo", "y"))


def solution(mesh):
    wide = Mesh(mesh.devices.reshape(SIZES), AXES)
    seq, vocab = ("z_hi", "y"), ("z_lo", "x")
    by_cols = P(seq, vocab + ("sect",))
    by_row = P(seq)
    return jax.shard_map(
        body,
        mesh=wide,
        in_specs=(P(seq, None), by_cols, P(seq + ("sect",), vocab), by_row, by_row, by_row),
        out_specs=(by_cols, P(seq, None), by_cols, by_row, by_row),
        check_vma=False,
    )
```

```python
import jax
import jax.numpy as jnp
from jax import lax
from jax.sharding import Mesh, PartitionSpec as P

CLIP_RATIO = 2.0
AXES = ("sect", "z_lo", "x", "z_hi", "y")
SIZES = (2, 4, 4, 2, 4)
SPLIT = ("sect", "z_lo", "x")
PAIR = [(0, 1), (1, 0)]


def spread(values, axes):
    count = lax.axis_size(axes)
    return lax.all_to_all(
        jnp.broadcast_to(values[None], (count,) + values.shape), axes, 0, 0, tiled=True
    )


def shift(values, axis, step):
    count = lax.axis_size(axis)
    return lax.ppermute(values, axis, [(i, (i + step) % count) for i in range(count)])


def after(values, earlier):
    return values + (earlier[(0,) * earlier.ndim] * 0).astype(values.dtype)


def in_order(first, later, at, start=0):
    count = len(later) + 1
    held = jnp.full((count,) + first.shape, start, first.dtype)
    for step, part in enumerate([first] + later):
        held = lax.dynamic_update_index_in_dim(held, part, lax.rem(at + count - step, count), 0)
    return held


def contract_cols(left_side, right_side):
    return lax.dot_general(
        left_side, right_side, (((1,), (1,)), ((), ())), preferred_element_type=jnp.float32
    )


def combine(every):
    student_max = jnp.max(every[:, 0], axis=0)
    teacher_max = jnp.max(every[:, 1], axis=0)
    lower = every[:, 0] - student_max
    scale = jnp.exp(lower)
    return jnp.stack(
        [
            student_max,
            teacher_max,
            jnp.sum(every[:, 2] * scale, axis=0),
            jnp.sum((every[:, 3] + every[:, 2] * lower) * scale, axis=0),
            jnp.sum(every[:, 4] * scale, axis=0),
            jnp.sum(every[:, 5] * jnp.exp(every[:, 1] - teacher_max), axis=0),
            jnp.sum(every[:, 6], axis=0),
            jnp.zeros_like(student_max),
        ]
    )


def body(hidden, head_weight, teacher_logits, sampled_ids, behaviour_logprob, valid_mask):
    width_part, col_count = head_weight.shape
    sect, z_lo, x_at, z_hi, y_at = (lax.axis_index(name) for name in AXES)
    quarter = col_count // 4
    half = 4 * width_part
    f32, bf16 = jnp.float32, jnp.bfloat16

    piece = lax.dynamic_slice_in_dim(hidden, 64 * sect + 16 * x_at, 16, axis=0)
    far_piece = lax.ppermute(
        lax.dynamic_slice_in_dim(piece, half * (1 - z_hi), half, axis=1), "z_hi", PAIR
    )
    near_piece = lax.dynamic_slice_in_dim(piece, half * z_hi, half, axis=1)

    weight_parts = head_weight.T.reshape(4, quarter, width_part)

    def weight_for(step):
        return lax.dynamic_index_in_dim(weight_parts, lax.rem(y_at + step, 4), 0, keepdims=False)

    weight_half = in_order(
        weight_for(0), [shift(weight_for(step), "y", step) for step in (1, 2, 3)], y_at
    )

    def logits_of(values):
        return sum(
            contract_cols(
                weight_half[k],
                lax.slice_in_dim(values, k * width_part, (k + 1) * width_part, axis=1),
            )
            for k in range(4)
        )

    def turned(values, axis):
        first, second = jnp.split(values, 2, axis=axis)
        return jnp.where(sect == 0, values, jnp.concatenate([second, first], axis=axis))

    pieces = spread(spread(jnp.stack([far_piece, near_piece]), "y"), "x")
    other_pieces = lax.ppermute(pieces, "sect", PAIR)
    far_halves = [kept[:, :, 0].reshape(256, half) for kept in (pieces, other_pieces)]
    near_halves = [kept[:, :, 1].reshape(256, half) for kept in (pieces, other_pieces)]
    given_logits = [logits_of(values) for values in far_halves]
    far_logits = [lax.ppermute(values, "z_hi", PAIR) for values in given_logits]
    far_rows = jnp.concatenate(far_halves)
    near_rows = jnp.concatenate(near_halves)
    logits = jnp.concatenate(
        [
            logits_of(near_halves[0]) + after(far_logits[0], given_logits[1]),
            logits_of(near_halves[1]) + far_logits[1],
        ],
        axis=1,
    )

    teacher = lax.all_to_all(
        teacher_logits.reshape(64, 8, quarter).transpose(1, 0, 2), ("sect", "y"), 0, 0, tiled=True
    )
    teacher = teacher.reshape(2, 4, 4, 16, quarter)
    teacher = jnp.stack(
        [lax.dynamic_index_in_dim(teacher, at, 0, keepdims=False) for at in (sect, 1 - sect)]
    )
    teacher = teacher.transpose(0, 2, 1, 3, 4).reshape(512, quarter).T.astype(f32)

    rows = jnp.stack(
        [sampled_ids.astype(f32), behaviour_logprob, valid_mask.astype(f32)]
        + [jnp.zeros_like(behaviour_logprob)] * 5
    )
    rows = spread(after(rows, given_logits[1]), "y")
    near_count = jnp.sum(rows[:, 2])
    valid_count = near_count + lax.ppermute(
        jnp.broadcast_to(near_count, (8, 128)), "z_hi", PAIR
    )[0, 0]
    rows = rows[:, :3].reshape(4, 3, 2, 4, 16).transpose(1, 2, 3, 0, 4)
    rows = turned(rows, 1).reshape(3, 512)
    ids, behaviour, valid = rows[0].astype(jnp.int32), rows[1], rows[2]

    first_col = (((z_lo * 4 + x_at) * 2 + sect) * 4 + y_at) * quarter
    matches = lax.broadcasted_iota(jnp.int32, logits.shape, 0) == ids - first_col
    own_max = jnp.max(logits, axis=0)
    own_teacher_max = jnp.max(teacher, axis=0)
    own_shifted = logits - own_max
    own_powers = jnp.exp(own_shifted)
    own = jnp.stack(
        [
            own_max,
            own_teacher_max,
            jnp.sum(own_powers, axis=0),
            jnp.sum(own_powers * own_shifted, axis=0),
            jnp.sum(own_powers * teacher, axis=0),
            jnp.sum(jnp.exp(teacher - own_teacher_max), axis=0),
            jnp.sum(jnp.where(matches, logits, 0.0), axis=0),
            jnp.zeros_like(own_max),
        ]
    )
    own = turned(after(own, valid_count), 1)
    for axes in STAGES:
        own = combine(spread(own, axes))
    own = turned(own, 1)
    student_max, teacher_max, student_sum, shifted_sum, teacher_mix, teacher_sum, sampled_logit = (
        own[i] for i in range(7)
    )
    log_student = jnp.log(student_sum)
    student_lse = student_max + log_student
    teacher_lse = teacher_max + jnp.log(teacher_sum)
    entropy = log_student - shifted_sum / student_sum
    token_kl = shifted_sum / student_sum - log_student - teacher_mix / student_sum + teacher_lse
    ratio_weight = jnp.minimum(jnp.exp(sampled_logit - student_lse - behaviour), CLIP_RATIO)
    row_factor = valid * ratio_weight / valid_count
    near_grad = (
        row_factor
        * (jnp.exp(logits - student_max) / student_sum)
        * (logits - student_lse - (teacher - teacher_lse) - token_kl)
    ).astype(bf16)

    def own_rows(values):
        kept = turned(values.reshape(2, 4, 4, 16), 0)
        return lax.dynamic_index_in_dim(kept, y_at, axis=2, keepdims=False).reshape(128)

    cut = quarter // 2

    def product(step, grads, start=0):
        held = lax.dynamic_index_in_dim(
            weight_parts, lax.rem(y_at + step, 4), 0, keepdims=False
        )[start : start + grads.shape[0]]
        return lax.dot_general(
            grads, held, (((0,), (0,)), ((), ())), preferred_element_type=f32
        )

    def ring(values, ready=None):
        back, ahead = shift(values, "y", 1), shift(values, "y", 3)
        sent = (back[:cut], ahead[cut:])
        if ready is not None:
            sent = tuple(part + (ready[:cut, :512] * 0).astype(bf16) for part in sent)
        top, bottom = shift(sent[0], "y", 1), shift(sent[1], "y", 3)
        part = product(0, values) + product(3, back) + product(1, ahead)
        part = part + product(2, top) + product(2, bottom, cut)
        opposite = jnp.concatenate([top, bottom])
        return [values, back, opposite, ahead], opposite, part

    far_grad = lax.ppermute(near_grad, "z_hi", PAIR)
    near_all, near_last, near_part = ring(near_grad)
    far_all, _, far_part = ring(far_grad + near_last * 0, near_part)
    kept = jnp.stack([near_part[:256], far_part[:256]]) + lax.ppermute(
        jnp.stack([near_part[256:], far_part[256:]]), "sect", PAIR
    )
    kept = kept.reshape(2, 4, 4, 16, width_part).transpose(2, 1, 0, 3, 4)
    kept = kept.reshape(16, 32, width_part)
    sums = lax.all_to_all(kept, ("z_lo", "x"), 0, 0, tiled=True)
    sums = jnp.sum(sums, axis=0).astype(bf16)

    nothing = (kept[0, 0, 0] * 0).astype(bf16)
    near_all = in_order(near_all[0], near_all[1:], y_at, nothing)
    far_all = in_order(far_all[0], far_all[1:], y_at, nothing)

    token = lax.broadcasted_iota(jnp.int32, (128, 512), 0)
    place = ((token // 64 ^ sect) * 4 + token // 16 % 4) * 64 + y_at * 16 + token % 16
    chosen = (place == lax.broadcasted_iota(jnp.int32, (128, 512), 1)).astype(bf16)
    chosen = chosen + (kept[:4, :, :512].reshape(128, 512) * 0).astype(bf16)
    logit_grad = contract_cols(chosen, near_all.reshape(col_count, 512)).astype(bf16)

    def weight_part(rows_in, grads):
        held = lax.dynamic_slice_in_dim(rows_in, width_part * y_at, width_part, axis=1)
        held = held + (kept.reshape(512, width_part) * 0).astype(bf16)
        return jnp.dot(grads.reshape(col_count, 512), held, preferred_element_type=f32)

    weight_grad = (weight_part(near_rows, near_all) + weight_part(far_rows, far_all)).astype(bf16).T
    sums = sums + weight_grad[:32, :width_part] * 0 + logit_grad[:32, :width_part] * 0

    def handed_over(values, flip):
        moves = [
            ((j * 2 + z) * 4 + k, (k * 2 + (z ^ flip)) * 4 + j)
            for j in range(4)
            for z in range(2)
            for k in range(4)
        ]
        return lax.ppermute(values, ("z_lo", "z_hi", "y"), moves)

    near_sum, far_sum = handed_over(sums[:16], 0), handed_over(sums[16:], 1)
    both = jnp.where(
        z_hi == 0, jnp.concatenate([near_sum, far_sum]), jnp.concatenate([far_sum, near_sum])
    )
    mine = spread(both, ("z_lo", "x")).reshape(4, 4, 2, 16, width_part)
    mine = jnp.concatenate(
        [mine[k, :, z].reshape(64, width_part) for z in range(2) for k in range(4)], axis=1
    )
    hidden_grad = lax.dynamic_update_index_in_dim(
        jnp.stack([mine, mine]), lax.ppermute(mine, "sect", PAIR), 1 - sect, 0
    ).reshape(128, 8 * width_part)
    return (
        logit_grad,
        hidden_grad,
        weight_grad,
        own_rows(entropy),
        own_rows(token_kl),
    )


STAGES = (("sect", "x"), ("z_lo", "y"))


def solution(mesh):
    wide = Mesh(mesh.devices.reshape(SIZES), AXES)
    seq, vocab = ("z_hi", "y"), ("z_lo", "x")
    by_cols = P(seq, vocab + ("sect",))
    by_row = P(seq)
    return jax.shard_map(
        body,
        mesh=wide,
        in_specs=(P(seq, None), by_cols, P(seq + ("sect",), vocab), by_row, by_row, by_row),
        out_specs=(by_cols, P(seq, None), by_cols, by_row, by_row),
        check_vma=False,
    )
```

```python
import jax
import jax.numpy as jnp
from jax import lax
from jax.sharding import Mesh, PartitionSpec as P

CLIP_RATIO = 2.0
AXES = ("sect", "z_lo", "x", "z_hi", "y")
SIZES = (2, 4, 4, 2, 4)
SPLIT = ("sect", "z_lo", "x")
PAIR = [(0, 1), (1, 0)]


def spread(values, axes):
    count = lax.axis_size(axes)
    return lax.all_to_all(
        jnp.broadcast_to(values[None], (count,) + values.shape), axes, 0, 0, tiled=True
    )


def shift(values, axis, step):
    count = lax.axis_size(axis)
    return lax.ppermute(values, axis, [(i, (i + step) % count) for i in range(count)])


def after(values, earlier):
    return values + (earlier[(0,) * earlier.ndim] * 0).astype(values.dtype)


def in_order(first, later, at, start=0):
    count = len(later) + 1
    held = jnp.full((count,) + first.shape, start, first.dtype)
    for step, part in enumerate([first] + later):
        held = lax.dynamic_update_index_in_dim(held, part, lax.rem(at + count - step, count), 0)
    return held


def contract_cols(left_side, right_side):
    return lax.dot_general(
        left_side, right_side, (((1,), (1,)), ((), ())), preferred_element_type=jnp.float32
    )


def combine(every):
    student_max = jnp.max(every[:, 0], axis=0)
    teacher_max = jnp.max(every[:, 1], axis=0)
    lower = every[:, 0] - student_max
    scale = jnp.exp(lower)
    return jnp.stack(
        [
            student_max,
            teacher_max,
            jnp.sum(every[:, 2] * scale, axis=0),
            jnp.sum((every[:, 3] + every[:, 2] * lower) * scale, axis=0),
            jnp.sum(every[:, 4] * scale, axis=0),
            jnp.sum(every[:, 5] * jnp.exp(every[:, 1] - teacher_max), axis=0),
            jnp.sum(every[:, 6], axis=0),
            jnp.zeros_like(student_max),
        ]
    )


def body(hidden, head_weight, teacher_logits, sampled_ids, behaviour_logprob, valid_mask):
    width_part, col_count = head_weight.shape
    sect, z_lo, x_at, z_hi, y_at = (lax.axis_index(name) for name in AXES)
    quarter = col_count // 4
    half = 4 * width_part
    f32, bf16 = jnp.float32, jnp.bfloat16

    piece = lax.dynamic_slice_in_dim(hidden, 64 * sect + 16 * x_at, 16, axis=0)
    far_piece = lax.ppermute(
        lax.dynamic_slice_in_dim(piece, half * (1 - z_hi), half, axis=1), "z_hi", PAIR
    )
    near_piece = lax.dynamic_slice_in_dim(piece, half * z_hi, half, axis=1)

    weight_parts = head_weight.T.reshape(4, quarter, width_part)

    def weight_for(step):
        return lax.dynamic_index_in_dim(weight_parts, lax.rem(y_at + step, 4), 0, keepdims=False)

    def logits_of(values):
        return sum(
            contract_cols(
                weight_half[k],
                lax.slice_in_dim(values, k * width_part, (k + 1) * width_part, axis=1),
            )
            for k in range(4)
        )

    def turned(values, axis):
        first, second = jnp.split(values, 2, axis=axis)
        return jnp.where(sect == 0, values, jnp.concatenate([second, first], axis=axis))

    rows = jnp.stack(
        [sampled_ids.astype(f32), behaviour_logprob, valid_mask.astype(f32)]
        + [jnp.zeros_like(behaviour_logprob)] * 5
    )
    rows = spread(rows, "y")
    pieces = spread(after(jnp.stack([far_piece, near_piece]), rows), "y")
    near_count = jnp.sum(rows[:, 2])
    valid_count = near_count + lax.ppermute(
        jnp.broadcast_to(near_count, (8, 128)), "z_hi", PAIR
    )[0, 0]
    rows = rows[:, :3].reshape(4, 3, 2, 4, 16).transpose(1, 2, 3, 0, 4)
    rows = turned(rows, 1).reshape(3, 512)
    ids, behaviour, valid = rows[0].astype(jnp.int32), rows[1], rows[2]

    sent = [weight_for(step) for step in (1, 2, 3)]
    for values in sent:
        pieces = after(pieces, values)
    pieces = spread(pieces, "x")
    weight_half = in_order(
        weight_for(0), [shift(values, "y", step) for step, values in enumerate(sent, 1)], y_at
    )
    teacher = lax.all_to_all(
        after(teacher_logits, pieces).reshape(64, 8, quarter).transpose(1, 0, 2),
        ("sect", "y"),
        0,
        0,
        tiled=True,
    )
    other_pieces = lax.ppermute(pieces, "sect", PAIR)
    far_halves = [kept[:, :, 0].reshape(256, half) for kept in (pieces, other_pieces)]
    near_halves = [kept[:, :, 1].reshape(256, half) for kept in (pieces, other_pieces)]
    far_halves[0] = after(far_halves[0], teacher) + (valid_count * 0).astype(bf16)
    given_logits = [logits_of(values) for values in far_halves]
    far_logits = [lax.ppermute(values, "z_hi", PAIR) for values in given_logits]
    far_rows = jnp.concatenate(far_halves)
    near_rows = jnp.concatenate(near_halves)
    logits = jnp.concatenate(
        [
            logits_of(near_halves[0]) + after(far_logits[0], given_logits[1]),
            logits_of(near_halves[1]) + far_logits[1],
        ],
        axis=1,
    )

    teacher = teacher.reshape(2, 4, 4, 16, quarter)
    teacher = jnp.stack(
        [lax.dynamic_index_in_dim(teacher, at, 0, keepdims=False) for at in (sect, 1 - sect)]
    )
    teacher = teacher.transpose(0, 2, 1, 3, 4).reshape(512, quarter).T.astype(f32)

    first_col = (((z_lo * 4 + x_at) * 2 + sect) * 4 + y_at) * quarter
    matches = lax.broadcasted_iota(jnp.int32, logits.shape, 0) == ids - first_col
    own_max = jnp.max(logits, axis=0)
    own_teacher_max = jnp.max(teacher, axis=0)
    own_shifted = logits - own_max
    own_powers = jnp.exp(own_shifted)
    own = jnp.stack(
        [
            own_max,
            own_teacher_max,
            jnp.sum(own_powers, axis=0),
            jnp.sum(own_powers * own_shifted, axis=0),
            jnp.sum(own_powers * teacher, axis=0),
            jnp.sum(jnp.exp(teacher - own_teacher_max), axis=0),
            jnp.sum(jnp.where(matches, logits, 0.0), axis=0),
            jnp.zeros_like(own_max),
        ]
    )
    own = turned(own, 1)
    for axes in STAGES:
        own = combine(spread(own, axes))
    own = turned(own, 1)
    student_max, teacher_max, student_sum, shifted_sum, teacher_mix, teacher_sum, sampled_logit = (
        own[i] for i in range(7)
    )
    log_student = jnp.log(student_sum)
    student_lse = student_max + log_student
    teacher_lse = teacher_max + jnp.log(teacher_sum)
    entropy = log_student - shifted_sum / student_sum
    token_kl = shifted_sum / student_sum - log_student - teacher_mix / student_sum + teacher_lse
    ratio_weight = jnp.minimum(jnp.exp(sampled_logit - student_lse - behaviour), CLIP_RATIO)
    row_factor = valid * ratio_weight / valid_count
    near_grad = (
        row_factor
        * (jnp.exp(logits - student_max) / student_sum)
        * (logits - student_lse - (teacher - teacher_lse) - token_kl)
    ).astype(bf16)

    def own_rows(values):
        kept = turned(values.reshape(2, 4, 4, 16), 0)
        return lax.dynamic_index_in_dim(kept, y_at, axis=2, keepdims=False).reshape(128)

    cut = quarter // 2

    def product(step, grads, start=0):
        held = lax.dynamic_index_in_dim(
            weight_parts, lax.rem(y_at + step, 4), 0, keepdims=False
        )[start : start + grads.shape[0]]
        return lax.dot_general(
            grads, held, (((0,), (0,)), ((), ())), preferred_element_type=f32
        )

    def ring(values, ready=None):
        back, ahead = shift(values, "y", 1), shift(values, "y", 3)
        sent = (back[:cut], ahead[cut:])
        if ready is not None:
            sent = tuple(part + (ready[:cut, :512] * 0).astype(bf16) for part in sent)
        top, bottom = shift(sent[0], "y", 1), shift(sent[1], "y", 3)
        part = product(0, values) + product(3, back) + product(1, ahead)
        part = part + product(2, top) + product(2, bottom, cut)
        opposite = jnp.concatenate([top, bottom])
        return [values, back, opposite, ahead], opposite, part

    far_grad = lax.ppermute(near_grad, "z_hi", PAIR)
    near_all, near_last, near_part = ring(near_grad)
    far_all, _, far_part = ring(far_grad + near_last * 0, near_part)
    kept = jnp.stack([near_part[:256], far_part[:256]]) + lax.ppermute(
        jnp.stack([near_part[256:], far_part[256:]]), "sect", PAIR
    )
    kept = kept.reshape(2, 4, 4, 16, width_part).transpose(2, 1, 0, 3, 4)
    kept = kept.reshape(16, 32, width_part)
    sums = lax.all_to_all(kept, ("z_lo", "x"), 0, 0, tiled=True)
    sums = jnp.sum(sums, axis=0).astype(bf16)

    nothing = (kept[0, 0, 0] * 0).astype(bf16)
    near_all = in_order(near_all[0], near_all[1:], y_at, nothing)
    far_all = in_order(far_all[0], far_all[1:], y_at, nothing)

    token = lax.broadcasted_iota(jnp.int32, (128, 512), 0)
    place = ((token // 64 ^ sect) * 4 + token // 16 % 4) * 64 + y_at * 16 + token % 16
    chosen = (place == lax.broadcasted_iota(jnp.int32, (128, 512), 1)).astype(bf16)
    chosen = chosen + (kept[:4, :, :512].reshape(128, 512) * 0).astype(bf16)
    logit_grad = contract_cols(chosen, near_all.reshape(col_count, 512)).astype(bf16)

    def weight_part(rows_in, grads):
        held = lax.dynamic_slice_in_dim(rows_in, width_part * y_at, width_part, axis=1)
        held = held + (kept.reshape(512, width_part) * 0).astype(bf16)
        return jnp.dot(grads.reshape(col_count, 512), held, preferred_element_type=f32)

    weight_grad = (weight_part(near_rows, near_all) + weight_part(far_rows, far_all)).astype(bf16).T
    sums = sums + weight_grad[:32, :width_part] * 0 + logit_grad[:32, :width_part] * 0

    def handed_over(values, flip):
        moves = [
            ((j * 2 + z) * 4 + k, (k * 2 + (z ^ flip)) * 4 + j)
            for j in range(4)
            for z in range(2)
            for k in range(4)
        ]
        return lax.ppermute(values, ("z_lo", "z_hi", "y"), moves)

    near_sum, far_sum = handed_over(sums[:16], 0), handed_over(sums[16:], 1)
    both = jnp.where(
        z_hi == 0, jnp.concatenate([near_sum, far_sum]), jnp.concatenate([far_sum, near_sum])
    )
    mine = spread(both, ("z_lo", "x")).reshape(4, 4, 2, 16, width_part)
    mine = jnp.concatenate(
        [mine[k, :, z].reshape(64, width_part) for z in range(2) for k in range(4)], axis=1
    )
    hidden_grad = lax.dynamic_update_index_in_dim(
        jnp.stack([mine, mine]), lax.ppermute(mine, "sect", PAIR), 1 - sect, 0
    ).reshape(128, 8 * width_part)
    return (
        logit_grad,
        hidden_grad,
        weight_grad,
        own_rows(entropy),
        own_rows(token_kl),
    )


STAGES = (("sect", "x"), ("z_lo", "y"))


def solution(mesh):
    wide = Mesh(mesh.devices.reshape(SIZES), AXES)
    seq, vocab = ("z_hi", "y"), ("z_lo", "x")
    by_cols = P(seq, vocab + ("sect",))
    by_row = P(seq)
    return jax.shard_map(
        body,
        mesh=wide,
        in_specs=(P(seq, None), by_cols, P(seq + ("sect",), vocab), by_row, by_row, by_row),
        out_specs=(by_cols, P(seq, None), by_cols, by_row, by_row),
        check_vma=False,
    )
```

```python
import jax
import jax.numpy as jnp
from jax import lax
from jax.sharding import Mesh, PartitionSpec as P

CLIP_RATIO = 2.0
AXES = ("sect", "z_lo", "x", "z_hi", "y")
SIZES = (2, 4, 4, 2, 4)
SPLIT = ("sect", "z_lo", "x")
PAIR = [(0, 1), (1, 0)]


def spread(values, axes):
    count = lax.axis_size(axes)
    return lax.all_to_all(
        jnp.broadcast_to(values[None], (count,) + values.shape), axes, 0, 0, tiled=True
    )


def shift(values, axis, step):
    count = lax.axis_size(axis)
    return lax.ppermute(values, axis, [(i, (i + step) % count) for i in range(count)])


def after(values, earlier):
    return values + (earlier[(0,) * earlier.ndim] * 0).astype(values.dtype)


def in_order(first, later, at, start=0):
    count = len(later) + 1
    held = jnp.full((count,) + first.shape, start, first.dtype)
    for step, part in enumerate([first] + later):
        held = lax.dynamic_update_index_in_dim(held, part, lax.rem(at + count - step, count), 0)
    return held


def contract_cols(left_side, right_side):
    return lax.dot_general(
        left_side, right_side, (((1,), (1,)), ((), ())), preferred_element_type=jnp.float32
    )


def combine(every):
    student_max = jnp.max(every[:, 0], axis=0)
    teacher_max = jnp.max(every[:, 1], axis=0)
    lower = every[:, 0] - student_max
    scale = jnp.exp(lower)
    return jnp.stack(
        [
            student_max,
            teacher_max,
            jnp.sum(every[:, 2] * scale, axis=0),
            jnp.sum((every[:, 3] + every[:, 2] * lower) * scale, axis=0),
            jnp.sum(every[:, 4] * scale, axis=0),
            jnp.sum(every[:, 5] * jnp.exp(every[:, 1] - teacher_max), axis=0),
            jnp.sum(every[:, 6], axis=0),
            jnp.zeros_like(student_max),
        ]
    )


def body(hidden, head_weight, teacher_logits, sampled_ids, behaviour_logprob, valid_mask):
    width_part, col_count = head_weight.shape
    sect, z_lo, x_at, z_hi, y_at = (lax.axis_index(name) for name in AXES)
    quarter = col_count // 4
    half = 4 * width_part
    f32, bf16 = jnp.float32, jnp.bfloat16

    piece = lax.dynamic_slice_in_dim(hidden, 64 * sect + 16 * x_at, 16, axis=0)
    far_piece = lax.ppermute(
        lax.dynamic_slice_in_dim(piece, half * (1 - z_hi), half, axis=1), "z_hi", PAIR
    )
    near_piece = lax.dynamic_slice_in_dim(piece, half * z_hi, half, axis=1)

    weight_parts = head_weight.T.reshape(4, quarter, width_part)

    def weight_for(step):
        return lax.dynamic_index_in_dim(weight_parts, lax.rem(y_at + step, 4), 0, keepdims=False)

    def logits_of(values):
        return sum(
            contract_cols(
                weight_half[k],
                lax.slice_in_dim(values, k * width_part, (k + 1) * width_part, axis=1),
            )
            for k in range(4)
        )

    def turned(values, axis):
        first, second = jnp.split(values, 2, axis=axis)
        return jnp.where(sect == 0, values, jnp.concatenate([second, first], axis=axis))

    rows = jnp.stack(
        [sampled_ids.astype(f32), behaviour_logprob, valid_mask.astype(f32)]
        + [jnp.zeros_like(behaviour_logprob)] * 5
    )
    rows = spread(rows, "y")
    pieces = spread(after(jnp.stack([far_piece, near_piece]), rows), "y")
    near_count = jnp.sum(rows[:, 2])
    valid_count = near_count + lax.ppermute(
        jnp.broadcast_to(near_count, (8, 128)), "z_hi", PAIR
    )[0, 0]
    rows = rows[:, :3].reshape(4, 3, 2, 4, 16).transpose(1, 2, 3, 0, 4)
    rows = turned(rows, 1).reshape(3, 512)
    ids, behaviour, valid = rows[0].astype(jnp.int32), rows[1], rows[2]

    sent = [weight_for(step) for step in (1, 2, 3)]
    for values in sent:
        pieces = after(pieces, values)
    pieces = spread(pieces, "x")
    weight_half = in_order(
        weight_for(0), [shift(values, "y", step) for step, values in enumerate(sent, 1)], y_at
    )
    other_pieces = lax.ppermute(pieces, "sect", PAIR)
    far_halves = [kept[:, :, 0].reshape(256, half) for kept in (pieces, other_pieces)]
    near_halves = [kept[:, :, 1].reshape(256, half) for kept in (pieces, other_pieces)]
    far_halves[0] = far_halves[0] + (valid_count * 0).astype(bf16)
    given_logits = [logits_of(values) for values in far_halves]
    far_logits = [lax.ppermute(values, "z_hi", PAIR) for values in given_logits]
    far_rows = jnp.concatenate(far_halves)
    near_rows = jnp.concatenate(near_halves)
    logits = jnp.concatenate(
        [
            logits_of(near_halves[0]) + after(far_logits[0], given_logits[1]),
            logits_of(near_halves[1]) + far_logits[1],
        ],
        axis=1,
    )

    teacher = lax.all_to_all(
        after(teacher_logits, given_logits[1]).reshape(64, 8, quarter).transpose(1, 0, 2),
        ("sect", "y"),
        0,
        0,
        tiled=True,
    )
    teacher = teacher.reshape(2, 4, 4, 16, quarter)
    teacher = jnp.stack(
        [lax.dynamic_index_in_dim(teacher, at, 0, keepdims=False) for at in (sect, 1 - sect)]
    )
    teacher = teacher.transpose(0, 2, 1, 3, 4).reshape(512, quarter).T.astype(f32)

    first_col = (((z_lo * 4 + x_at) * 2 + sect) * 4 + y_at) * quarter
    matches = lax.broadcasted_iota(jnp.int32, logits.shape, 0) == ids - first_col
    own_max = jnp.max(logits, axis=0)
    own_teacher_max = jnp.max(teacher, axis=0)
    own_shifted = logits - own_max
    own_powers = jnp.exp(own_shifted)
    own = jnp.stack(
        [
            own_max,
            own_teacher_max,
            jnp.sum(own_powers, axis=0),
            jnp.sum(own_powers * own_shifted, axis=0),
            jnp.sum(own_powers * teacher, axis=0),
            jnp.sum(jnp.exp(teacher - own_teacher_max), axis=0),
            jnp.sum(jnp.where(matches, logits, 0.0), axis=0),
            jnp.zeros_like(own_max),
        ]
    )
    own = turned(own, 1)
    for axes in STAGES:
        own = combine(spread(own, axes))
    own = turned(own, 1)
    student_max, teacher_max, student_sum, shifted_sum, teacher_mix, teacher_sum, sampled_logit = (
        own[i] for i in range(7)
    )
    log_student = jnp.log(student_sum)
    student_lse = student_max + log_student
    teacher_lse = teacher_max + jnp.log(teacher_sum)
    entropy = log_student - shifted_sum / student_sum
    token_kl = shifted_sum / student_sum - log_student - teacher_mix / student_sum + teacher_lse
    ratio_weight = jnp.minimum(jnp.exp(sampled_logit - student_lse - behaviour), CLIP_RATIO)
    row_factor = valid * ratio_weight / valid_count
    near_grad = (
        row_factor
        * (jnp.exp(logits - student_max) / student_sum)
        * (logits - student_lse - (teacher - teacher_lse) - token_kl)
    ).astype(bf16)

    def own_rows(values):
        kept = turned(values.reshape(2, 4, 4, 16), 0)
        return lax.dynamic_index_in_dim(kept, y_at, axis=2, keepdims=False).reshape(128)

    cut = quarter // 2

    def product(step, grads, start=0):
        held = lax.dynamic_index_in_dim(
            weight_parts, lax.rem(y_at + step, 4), 0, keepdims=False
        )[start : start + grads.shape[0]]
        return lax.dot_general(
            grads, held, (((0,), (0,)), ((), ())), preferred_element_type=f32
        )

    def ring(values, ready=None):
        back, ahead = shift(values, "y", 1), shift(values, "y", 3)
        sent = (back[:cut], ahead[cut:])
        if ready is not None:
            sent = tuple(part + (ready[:cut, :512] * 0).astype(bf16) for part in sent)
        top, bottom = shift(sent[0], "y", 1), shift(sent[1], "y", 3)
        part = product(0, values) + product(3, back) + product(1, ahead)
        part = part + product(2, top) + product(2, bottom, cut)
        opposite = jnp.concatenate([top, bottom])
        return [values, back, opposite, ahead], opposite, part

    far_grad = lax.ppermute(near_grad, "z_hi", PAIR)
    near_all, near_last, near_part = ring(near_grad)
    far_all, _, far_part = ring(far_grad + near_last * 0, near_part)
    kept = jnp.stack([near_part[:256], far_part[:256]]) + lax.ppermute(
        jnp.stack([near_part[256:], far_part[256:]]), "sect", PAIR
    )
    kept = kept.reshape(2, 4, 4, 16, width_part).transpose(2, 1, 0, 3, 4)
    kept = kept.reshape(16, 32, width_part)
    sums = lax.all_to_all(kept, ("z_lo", "x"), 0, 0, tiled=True)
    sums = jnp.sum(sums, axis=0).astype(bf16)

    nothing = (kept[0, 0, 0] * 0).astype(bf16)
    near_all = in_order(near_all[0], near_all[1:], y_at, nothing)
    far_all = in_order(far_all[0], far_all[1:], y_at, nothing)

    token = lax.broadcasted_iota(jnp.int32, (128, 512), 0)
    place = ((token // 64 ^ sect) * 4 + token // 16 % 4) * 64 + y_at * 16 + token % 16
    chosen = (place == lax.broadcasted_iota(jnp.int32, (128, 512), 1)).astype(bf16)
    chosen = chosen + (kept[:4, :, :512].reshape(128, 512) * 0).astype(bf16)
    logit_grad = contract_cols(chosen, near_all.reshape(col_count, 512)).astype(bf16)

    def weight_part(rows_in, grads):
        held = lax.dynamic_slice_in_dim(rows_in, width_part * y_at, width_part, axis=1)
        held = held + (kept.reshape(512, width_part) * 0).astype(bf16)
        return jnp.dot(grads.reshape(col_count, 512), held, preferred_element_type=f32)

    weight_grad = (weight_part(near_rows, near_all) + weight_part(far_rows, far_all)).astype(bf16).T
    sums = sums + weight_grad[:32, :width_part] * 0 + logit_grad[:32, :width_part] * 0

    def handed_over(values, flip):
        moves = [
            ((j * 2 + z) * 4 + k, (k * 2 + (z ^ flip)) * 4 + j)
            for j in range(4)
            for z in range(2)
            for k in range(4)
        ]
        return lax.ppermute(values, ("z_lo", "z_hi", "y"), moves)

    near_sum, far_sum = handed_over(sums[:16], 0), handed_over(sums[16:], 1)
    both = jnp.where(
        z_hi == 0, jnp.concatenate([near_sum, far_sum]), jnp.concatenate([far_sum, near_sum])
    )
    mine = spread(both, ("z_lo", "x")).reshape(4, 4, 2, 16, width_part)
    mine = jnp.concatenate(
        [mine[k, :, z].reshape(64, width_part) for z in range(2) for k in range(4)], axis=1
    )
    hidden_grad = lax.dynamic_update_index_in_dim(
        jnp.stack([mine, mine]), lax.ppermute(mine, "sect", PAIR), 1 - sect, 0
    ).reshape(128, 8 * width_part)
    return (
        logit_grad,
        hidden_grad,
        weight_grad,
        own_rows(entropy),
        own_rows(token_kl),
    )


STAGES = (("sect", "x"), ("z_lo", "y"))


def solution(mesh):
    wide = Mesh(mesh.devices.reshape(SIZES), AXES)
    seq, vocab = ("z_hi", "y"), ("z_lo", "x")
    by_cols = P(seq, vocab + ("sect",))
    by_row = P(seq)
    return jax.shard_map(
        body,
        mesh=wide,
        in_specs=(P(seq, None), by_cols, P(seq + ("sect",), vocab), by_row, by_row, by_row),
        out_specs=(by_cols, P(seq, None), by_cols, by_row, by_row),
        check_vma=False,
    )
```

```python
import jax
import jax.numpy as jnp
from jax import lax
from jax.sharding import Mesh, PartitionSpec as P

CLIP_RATIO = 2.0
AXES = ("sect", "z_lo", "x", "z_hi", "y")
SIZES = (2, 4, 4, 2, 4)
SPLIT = ("sect", "z_lo", "x")
PAIR = [(0, 1), (1, 0)]


def spread(values, axes):
    count = lax.axis_size(axes)
    return lax.all_to_all(
        jnp.broadcast_to(values[None], (count,) + values.shape), axes, 0, 0, tiled=True
    )


def shift(values, axis, step):
    count = lax.axis_size(axis)
    return lax.ppermute(values, axis, [(i, (i + step) % count) for i in range(count)])


def after(values, earlier):
    return values + (earlier[(0,) * earlier.ndim] * 0).astype(values.dtype)


def in_order(first, later, at, start=0):
    count = len(later) + 1
    held = jnp.full((count,) + first.shape, start, first.dtype)
    for step, part in enumerate([first] + later):
        held = lax.dynamic_update_index_in_dim(held, part, lax.rem(at + count - step, count), 0)
    return held


def contract_cols(left_side, right_side):
    return lax.dot_general(
        left_side, right_side, (((1,), (1,)), ((), ())), preferred_element_type=jnp.float32
    )


def combine(every):
    student_max = jnp.max(every[:, 0], axis=0)
    teacher_max = jnp.max(every[:, 1], axis=0)
    lower = every[:, 0] - student_max
    scale = jnp.exp(lower)
    return jnp.stack(
        [
            student_max,
            teacher_max,
            jnp.sum(every[:, 2] * scale, axis=0),
            jnp.sum((every[:, 3] + every[:, 2] * lower) * scale, axis=0),
            jnp.sum(every[:, 4] * scale, axis=0),
            jnp.sum(every[:, 5] * jnp.exp(every[:, 1] - teacher_max), axis=0),
            jnp.sum(every[:, 6], axis=0),
            jnp.zeros_like(student_max),
        ]
    )


def body(hidden, head_weight, teacher_logits, sampled_ids, behaviour_logprob, valid_mask):
    width_part, col_count = head_weight.shape
    sect, z_lo, x_at, z_hi, y_at = (lax.axis_index(name) for name in AXES)
    quarter = col_count // 4
    half = 4 * width_part
    f32, bf16 = jnp.float32, jnp.bfloat16

    piece = lax.dynamic_slice_in_dim(hidden, 64 * sect + 16 * x_at, 16, axis=0)
    far_piece = lax.ppermute(
        lax.dynamic_slice_in_dim(piece, half * (1 - z_hi), half, axis=1), "z_hi", PAIR
    )
    near_piece = lax.dynamic_slice_in_dim(piece, half * z_hi, half, axis=1)

    weight_parts = head_weight.T.reshape(4, quarter, width_part)

    def weight_for(step):
        return lax.dynamic_index_in_dim(weight_parts, lax.rem(y_at + step, 4), 0, keepdims=False)

    def logits_of(values):
        return sum(
            contract_cols(
                weight_half[k],
                lax.slice_in_dim(values, k * width_part, (k + 1) * width_part, axis=1),
            )
            for k in range(4)
        )

    def turned(values, axis):
        first, second = jnp.split(values, 2, axis=axis)
        return jnp.where(sect == 0, values, jnp.concatenate([second, first], axis=axis))

    pieces = spread(jnp.stack([far_piece, near_piece]), "y")
    mask = valid_mask.astype(f32)
    far_mask = lax.ppermute(mask, "z_hi", PAIR)
    sent = [weight_for(step) for step in (1, 2, 3)]
    pieces = spread(after(pieces, sent[0]), "x")
    weight_half = in_order(
        weight_for(0), [shift(values, "y", step) for step, values in enumerate(sent, 1)], y_at
    )
    other_pieces = lax.ppermute(pieces, "sect", PAIR)
    far_halves = [kept[:, :, 0].reshape(256, half) for kept in (pieces, other_pieces)]
    near_halves = [kept[:, :, 1].reshape(256, half) for kept in (pieces, other_pieces)]
    far_halves[0] = after(far_halves[0], far_mask)
    given_logits = [logits_of(values) for values in far_halves]
    far_logits = [lax.ppermute(values, "z_hi", PAIR) for values in given_logits]
    far_rows = jnp.concatenate(far_halves)
    near_rows = jnp.concatenate(near_halves)
    logits = jnp.concatenate(
        [
            logits_of(near_halves[0]) + after(far_logits[0], given_logits[1]),
            logits_of(near_halves[1]) + far_logits[1],
        ],
        axis=1,
    )

    rows = jnp.stack(
        [sampled_ids.astype(f32), behaviour_logprob, mask, far_mask]
        + [jnp.zeros_like(behaviour_logprob)] * 4
    )
    rows = spread(after(rows, given_logits[1]), "y")
    valid_count = jnp.sum(rows[:, 2:4])
    rows = rows[:, :3].reshape(4, 3, 2, 4, 16).transpose(1, 2, 3, 0, 4)
    rows = turned(rows, 1).reshape(3, 512)
    ids, behaviour, valid = rows[0].astype(jnp.int32), rows[1], rows[2]

    teacher = lax.all_to_all(
        after(teacher_logits, given_logits[1]).reshape(64, 8, quarter).transpose(1, 0, 2),
        ("sect", "y"),
        0,
        0,
        tiled=True,
    )
    teacher = teacher.reshape(2, 4, 4, 16, quarter)
    teacher = jnp.stack(
        [lax.dynamic_index_in_dim(teacher, at, 0, keepdims=False) for at in (sect, 1 - sect)]
    )
    teacher = teacher.transpose(0, 2, 1, 3, 4).reshape(512, quarter).T.astype(f32)

    first_col = (((z_lo * 4 + x_at) * 2 + sect) * 4 + y_at) * quarter
    matches = lax.broadcasted_iota(jnp.int32, logits.shape, 0) == ids - first_col
    own_max = jnp.max(logits, axis=0)
    own_teacher_max = jnp.max(teacher, axis=0)
    own_shifted = logits - own_max
    own_powers = jnp.exp(own_shifted)
    own = jnp.stack(
        [
            own_max,
            own_teacher_max,
            jnp.sum(own_powers, axis=0),
            jnp.sum(own_powers * own_shifted, axis=0),
            jnp.sum(own_powers * teacher, axis=0),
            jnp.sum(jnp.exp(teacher - own_teacher_max), axis=0),
            jnp.sum(jnp.where(matches, logits, 0.0), axis=0),
            jnp.zeros_like(own_max),
        ]
    )
    own = turned(own, 1)
    for axes in STAGES:
        own = combine(spread(own, axes))
    own = turned(own, 1)
    student_max, teacher_max, student_sum, shifted_sum, teacher_mix, teacher_sum, sampled_logit = (
        own[i] for i in range(7)
    )
    log_student = jnp.log(student_sum)
    student_lse = student_max + log_student
    teacher_lse = teacher_max + jnp.log(teacher_sum)
    entropy = log_student - shifted_sum / student_sum
    token_kl = shifted_sum / student_sum - log_student - teacher_mix / student_sum + teacher_lse
    ratio_weight = jnp.minimum(jnp.exp(sampled_logit - student_lse - behaviour), CLIP_RATIO)
    row_factor = valid * ratio_weight / valid_count
    near_grad = (
        row_factor
        * (jnp.exp(logits - student_max) / student_sum)
        * (logits - student_lse - (teacher - teacher_lse) - token_kl)
    ).astype(bf16)

    def own_rows(values):
        kept = turned(values.reshape(2, 4, 4, 16), 0)
        return lax.dynamic_index_in_dim(kept, y_at, axis=2, keepdims=False).reshape(128)

    cut = quarter // 2

    def product(step, grads, start=0):
        held = lax.dynamic_index_in_dim(
            weight_parts, lax.rem(y_at + step, 4), 0, keepdims=False
        )[start : start + grads.shape[0]]
        return lax.dot_general(
            grads, held, (((0,), (0,)), ((), ())), preferred_element_type=f32
        )

    def ring(values, ready=None):
        back, ahead = shift(values, "y", 1), shift(values, "y", 3)
        sent = (back[:cut], ahead[cut:])
        if ready is not None:
            sent = tuple(part + (ready[:cut, :512] * 0).astype(bf16) for part in sent)
        top, bottom = shift(sent[0], "y", 1), shift(sent[1], "y", 3)
        part = product(0, values) + product(3, back) + product(1, ahead)
        part = part + product(2, top) + product(2, bottom, cut)
        opposite = jnp.concatenate([top, bottom])
        return [values, back, opposite, ahead], opposite, part

    far_grad = lax.ppermute(near_grad, "z_hi", PAIR)
    near_all, near_last, near_part = ring(near_grad)
    far_all, _, far_part = ring(far_grad + near_last * 0, near_part)
    kept = jnp.stack([near_part[:256], far_part[:256]]) + lax.ppermute(
        jnp.stack([near_part[256:], far_part[256:]]), "sect", PAIR
    )
    kept = kept.reshape(2, 4, 4, 16, width_part).transpose(2, 1, 0, 3, 4)
    kept = kept.reshape(16, 32, width_part)
    sums = lax.all_to_all(kept, ("z_lo", "x"), 0, 0, tiled=True)
    sums = jnp.sum(sums, axis=0).astype(bf16)

    nothing = (kept[0, 0, 0] * 0).astype(bf16)
    near_all = in_order(near_all[0], near_all[1:], y_at, nothing)
    far_all = in_order(far_all[0], far_all[1:], y_at, nothing)

    token = lax.broadcasted_iota(jnp.int32, (128, 512), 0)
    place = ((token // 64 ^ sect) * 4 + token // 16 % 4) * 64 + y_at * 16 + token % 16
    chosen = (place == lax.broadcasted_iota(jnp.int32, (128, 512), 1)).astype(bf16)
    chosen = chosen + (kept[:4, :, :512].reshape(128, 512) * 0).astype(bf16)
    logit_grad = contract_cols(chosen, near_all.reshape(col_count, 512)).astype(bf16)

    def weight_part(rows_in, grads):
        held = lax.dynamic_slice_in_dim(rows_in, width_part * y_at, width_part, axis=1)
        held = held + (kept.reshape(512, width_part) * 0).astype(bf16)
        return jnp.dot(grads.reshape(col_count, 512), held, preferred_element_type=f32)

    weight_grad = (weight_part(near_rows, near_all) + weight_part(far_rows, far_all)).astype(bf16).T
    sums = sums + weight_grad[:32, :width_part] * 0 + logit_grad[:32, :width_part] * 0

    def handed_over(values, flip):
        moves = [
            ((j * 2 + z) * 4 + k, (k * 2 + (z ^ flip)) * 4 + j)
            for j in range(4)
            for z in range(2)
            for k in range(4)
        ]
        return lax.ppermute(values, ("z_lo", "z_hi", "y"), moves)

    near_sum, far_sum = handed_over(sums[:16], 0), handed_over(sums[16:], 1)
    both = jnp.where(
        z_hi == 0, jnp.concatenate([near_sum, far_sum]), jnp.concatenate([far_sum, near_sum])
    )
    mine = spread(both, ("z_lo", "x")).reshape(4, 4, 2, 16, width_part)
    mine = jnp.concatenate(
        [mine[k, :, z].reshape(64, width_part) for z in range(2) for k in range(4)], axis=1
    )
    hidden_grad = lax.dynamic_update_index_in_dim(
        jnp.stack([mine, mine]), lax.ppermute(mine, "sect", PAIR), 1 - sect, 0
    ).reshape(128, 8 * width_part)
    return (
        logit_grad,
        hidden_grad,
        weight_grad,
        own_rows(entropy),
        own_rows(token_kl),
    )


STAGES = (("sect", "x"), ("z_lo", "y"))


def solution(mesh):
    wide = Mesh(mesh.devices.reshape(SIZES), AXES)
    seq, vocab = ("z_hi", "y"), ("z_lo", "x")
    by_cols = P(seq, vocab + ("sect",))
    by_row = P(seq)
    return jax.shard_map(
        body,
        mesh=wide,
        in_specs=(P(seq, None), by_cols, P(seq + ("sect",), vocab), by_row, by_row, by_row),
        out_specs=(by_cols, P(seq, None), by_cols, by_row, by_row),
        check_vma=False,
    )
```

```python
import jax
import jax.numpy as jnp
from jax import lax
from jax.sharding import Mesh, PartitionSpec as P

CLIP_RATIO = 2.0
AXES = ("sect", "z_lo", "x", "z_hi", "y")
SIZES = (2, 4, 4, 2, 4)
SPLIT = ("sect", "z_lo", "x")
PAIR = [(0, 1), (1, 0)]


def spread(values, axes):
    count = lax.axis_size(axes)
    return lax.all_to_all(
        jnp.broadcast_to(values[None], (count,) + values.shape), axes, 0, 0, tiled=True
    )


def shift(values, axis, step):
    count = lax.axis_size(axis)
    return lax.ppermute(values, axis, [(i, (i + step) % count) for i in range(count)])


def after(values, earlier):
    return values + (earlier[(0,) * earlier.ndim] * 0).astype(values.dtype)


def in_order(first, later, at, start=0):
    count = len(later) + 1
    held = jnp.full((count,) + first.shape, start, first.dtype)
    for step, part in enumerate([first] + later):
        held = lax.dynamic_update_index_in_dim(held, part, lax.rem(at + count - step, count), 0)
    return held


def contract_cols(left_side, right_side):
    return lax.dot_general(
        left_side, right_side, (((1,), (1,)), ((), ())), preferred_element_type=jnp.float32
    )


def combine(every):
    student_max = jnp.max(every[:, 0], axis=0)
    teacher_max = jnp.max(every[:, 1], axis=0)
    lower = every[:, 0] - student_max
    scale = jnp.exp(lower)
    return jnp.stack(
        [
            student_max,
            teacher_max,
            jnp.sum(every[:, 2] * scale, axis=0),
            jnp.sum((every[:, 3] + every[:, 2] * lower) * scale, axis=0),
            jnp.sum(every[:, 4] * scale, axis=0),
            jnp.sum(every[:, 5] * jnp.exp(every[:, 1] - teacher_max), axis=0),
            jnp.sum(every[:, 6], axis=0),
            jnp.zeros_like(student_max),
        ]
    )


def body(hidden, head_weight, teacher_logits, sampled_ids, behaviour_logprob, valid_mask):
    width_part, col_count = head_weight.shape
    sect, z_lo, x_at, z_hi, y_at = (lax.axis_index(name) for name in AXES)
    quarter = col_count // 4
    half = 4 * width_part
    f32, bf16 = jnp.float32, jnp.bfloat16

    piece = lax.dynamic_slice_in_dim(hidden, 64 * sect + 16 * x_at, 16, axis=0)
    far_piece = lax.ppermute(
        lax.dynamic_slice_in_dim(piece, half * (1 - z_hi), half, axis=1), "z_hi", PAIR
    )
    near_piece = lax.dynamic_slice_in_dim(piece, half * z_hi, half, axis=1)

    weight_parts = head_weight.T.reshape(4, quarter, width_part)

    def weight_for(step):
        return lax.dynamic_index_in_dim(weight_parts, lax.rem(y_at + step, 4), 0, keepdims=False)

    def logits_of(values):
        return sum(
            contract_cols(
                weight_half[k],
                lax.slice_in_dim(values, k * width_part, (k + 1) * width_part, axis=1),
            )
            for k in range(4)
        )

    def turned(values, axis):
        first, second = jnp.split(values, 2, axis=axis)
        return jnp.where(sect == 0, values, jnp.concatenate([second, first], axis=axis))

    pieces = spread(jnp.stack([far_piece, near_piece]), "y")
    mask = valid_mask.astype(f32)
    far_mask = lax.ppermute(mask, "z_hi", PAIR)
    sent = [weight_for(step) for step in (1, 2, 3)]
    pieces = spread(after(pieces, sent[0]), "x")
    weight_half = in_order(
        weight_for(0), [shift(values, "y", step) for step, values in enumerate(sent, 1)], y_at
    )
    other_pieces = lax.ppermute(pieces, "sect", PAIR)
    far_halves = [kept[:, :, 0].reshape(256, half) for kept in (pieces, other_pieces)]
    near_halves = [kept[:, :, 1].reshape(256, half) for kept in (pieces, other_pieces)]
    far_halves[0] = after(far_halves[0], far_mask)
    given_logits = [logits_of(values) for values in far_halves]
    far_logits = [lax.ppermute(values, "z_hi", PAIR) for values in given_logits]
    far_rows = jnp.concatenate(far_halves)
    near_rows = jnp.concatenate(near_halves)
    logits = jnp.concatenate(
        [
            logits_of(near_halves[0]) + after(far_logits[0], given_logits[1]),
            logits_of(near_halves[1]) + far_logits[1],
        ],
        axis=1,
    )

    teacher = lax.all_to_all(
        after(teacher_logits, given_logits[1]).reshape(64, 8, quarter).transpose(1, 0, 2),
        ("sect", "y"),
        0,
        0,
        tiled=True,
    )
    rows = jnp.stack(
        [sampled_ids.astype(f32), behaviour_logprob, mask, far_mask]
        + [jnp.zeros_like(behaviour_logprob)] * 4
    )
    rows = spread(after(rows, teacher), "y")
    valid_count = jnp.sum(rows[:, 2:4])
    rows = rows[:, :3].reshape(4, 3, 2, 4, 16).transpose(1, 2, 3, 0, 4)
    rows = turned(rows, 1).reshape(3, 512)
    ids, behaviour, valid = rows[0].astype(jnp.int32), rows[1], rows[2]

    teacher = teacher.reshape(2, 4, 4, 16, quarter)
    teacher = jnp.stack(
        [lax.dynamic_index_in_dim(teacher, at, 0, keepdims=False) for at in (sect, 1 - sect)]
    )
    teacher = teacher.transpose(0, 2, 1, 3, 4).reshape(512, quarter).T.astype(f32)

    first_col = (((z_lo * 4 + x_at) * 2 + sect) * 4 + y_at) * quarter
    matches = lax.broadcasted_iota(jnp.int32, logits.shape, 0) == ids - first_col
    own_max = jnp.max(logits, axis=0)
    own_teacher_max = jnp.max(teacher, axis=0)
    own_shifted = logits - own_max
    own_powers = jnp.exp(own_shifted)
    own = jnp.stack(
        [
            own_max,
            own_teacher_max,
            jnp.sum(own_powers, axis=0),
            jnp.sum(own_powers * own_shifted, axis=0),
            jnp.sum(own_powers * teacher, axis=0),
            jnp.sum(jnp.exp(teacher - own_teacher_max), axis=0),
            jnp.sum(jnp.where(matches, logits, 0.0), axis=0),
            jnp.zeros_like(own_max),
        ]
    )
    own = turned(own, 1)
    for axes in STAGES:
        own = combine(spread(own, axes))
    own = turned(own, 1)
    student_max, teacher_max, student_sum, shifted_sum, teacher_mix, teacher_sum, sampled_logit = (
        own[i] for i in range(7)
    )
    log_student = jnp.log(student_sum)
    student_lse = student_max + log_student
    teacher_lse = teacher_max + jnp.log(teacher_sum)
    entropy = log_student - shifted_sum / student_sum
    token_kl = shifted_sum / student_sum - log_student - teacher_mix / student_sum + teacher_lse
    ratio_weight = jnp.minimum(jnp.exp(sampled_logit - student_lse - behaviour), CLIP_RATIO)
    row_factor = valid * ratio_weight / valid_count
    near_grad = (
        row_factor
        * (jnp.exp(logits - student_max) / student_sum)
        * (logits - student_lse - (teacher - teacher_lse) - token_kl)
    ).astype(bf16)

    def own_rows(values):
        kept = turned(values.reshape(2, 4, 4, 16), 0)
        return lax.dynamic_index_in_dim(kept, y_at, axis=2, keepdims=False).reshape(128)

    cut = quarter // 2

    def product(step, grads, start=0):
        held = lax.dynamic_index_in_dim(
            weight_parts, lax.rem(y_at + step, 4), 0, keepdims=False
        )[start : start + grads.shape[0]]
        return lax.dot_general(
            grads, held, (((0,), (0,)), ((), ())), preferred_element_type=f32
        )

    def ring(values, ready=None):
        back, ahead = shift(values, "y", 1), shift(values, "y", 3)
        sent = (back[:cut], ahead[cut:])
        if ready is not None:
            sent = tuple(part + (ready[:cut, :512] * 0).astype(bf16) for part in sent)
        top, bottom = shift(sent[0], "y", 1), shift(sent[1], "y", 3)
        part = product(0, values) + product(3, back) + product(1, ahead)
        part = part + product(2, top) + product(2, bottom, cut)
        opposite = jnp.concatenate([top, bottom])
        return [values, back, opposite, ahead], opposite, part

    far_grad = lax.ppermute(near_grad, "z_hi", PAIR)
    near_all, near_last, near_part = ring(near_grad)
    far_all, _, far_part = ring(far_grad + near_last * 0, near_part)
    kept = jnp.stack([near_part[:256], far_part[:256]]) + lax.ppermute(
        jnp.stack([near_part[256:], far_part[256:]]), "sect", PAIR
    )
    kept = kept.reshape(2, 4, 4, 16, width_part).transpose(2, 1, 0, 3, 4)
    kept = kept.reshape(16, 32, width_part)
    sums = lax.all_to_all(kept, ("z_lo", "x"), 0, 0, tiled=True)
    sums = jnp.sum(sums, axis=0).astype(bf16)

    nothing = (kept[0, 0, 0] * 0).astype(bf16)
    near_all = in_order(near_all[0], near_all[1:], y_at, nothing)
    far_all = in_order(far_all[0], far_all[1:], y_at, nothing)

    token = lax.broadcasted_iota(jnp.int32, (128, 512), 0)
    place = ((token // 64 ^ sect) * 4 + token // 16 % 4) * 64 + y_at * 16 + token % 16
    chosen = (place == lax.broadcasted_iota(jnp.int32, (128, 512), 1)).astype(bf16)
    chosen = chosen + (kept[:4, :, :512].reshape(128, 512) * 0).astype(bf16)
    logit_grad = contract_cols(chosen, near_all.reshape(col_count, 512)).astype(bf16)

    def weight_part(rows_in, grads):
        held = lax.dynamic_slice_in_dim(rows_in, width_part * y_at, width_part, axis=1)
        held = held + (kept.reshape(512, width_part) * 0).astype(bf16)
        return jnp.dot(grads.reshape(col_count, 512), held, preferred_element_type=f32)

    weight_grad = (weight_part(near_rows, near_all) + weight_part(far_rows, far_all)).astype(bf16).T
    sums = sums + weight_grad[:32, :width_part] * 0 + logit_grad[:32, :width_part] * 0

    def handed_over(values, flip):
        moves = [
            ((j * 2 + z) * 4 + k, (k * 2 + (z ^ flip)) * 4 + j)
            for j in range(4)
            for z in range(2)
            for k in range(4)
        ]
        return lax.ppermute(values, ("z_lo", "z_hi", "y"), moves)

    near_sum, far_sum = handed_over(sums[:16], 0), handed_over(sums[16:], 1)
    both = jnp.where(
        z_hi == 0, jnp.concatenate([near_sum, far_sum]), jnp.concatenate([far_sum, near_sum])
    )
    mine = spread(both, ("z_lo", "x")).reshape(4, 4, 2, 16, width_part)
    mine = jnp.concatenate(
        [mine[k, :, z].reshape(64, width_part) for z in range(2) for k in range(4)], axis=1
    )
    hidden_grad = lax.dynamic_update_index_in_dim(
        jnp.stack([mine, mine]), lax.ppermute(mine, "sect", PAIR), 1 - sect, 0
    ).reshape(128, 8 * width_part)
    return (
        logit_grad,
        hidden_grad,
        weight_grad,
        own_rows(entropy),
        own_rows(token_kl),
    )


STAGES = (("sect", "x"), ("z_lo", "y"))


def solution(mesh):
    wide = Mesh(mesh.devices.reshape(SIZES), AXES)
    seq, vocab = ("z_hi", "y"), ("z_lo", "x")
    by_cols = P(seq, vocab + ("sect",))
    by_row = P(seq)
    return jax.shard_map(
        body,
        mesh=wide,
        in_specs=(P(seq, None), by_cols, P(seq + ("sect",), vocab), by_row, by_row, by_row),
        out_specs=(by_cols, P(seq, None), by_cols, by_row, by_row),
        check_vma=False,
    )
```

```python
import jax
import jax.numpy as jnp
from jax import lax
from jax.sharding import Mesh, PartitionSpec as P

CLIP_RATIO = 2.0
AXES = ("sect", "z_lo", "x", "z_hi", "y")
SIZES = (2, 4, 4, 2, 4)
SPLIT = ("sect", "z_lo", "x")
PAIR = [(0, 1), (1, 0)]


def spread(values, axes):
    count = lax.axis_size(axes)
    return lax.all_to_all(
        jnp.broadcast_to(values[None], (count,) + values.shape), axes, 0, 0, tiled=True
    )


def shift(values, axis, step):
    count = lax.axis_size(axis)
    return lax.ppermute(values, axis, [(i, (i + step) % count) for i in range(count)])


def after(values, earlier):
    return values + (earlier[(0,) * earlier.ndim] * 0).astype(values.dtype)


def in_order(first, later, at, start=0):
    count = len(later) + 1
    held = jnp.full((count,) + first.shape, start, first.dtype)
    for step, part in enumerate([first] + later):
        held = lax.dynamic_update_index_in_dim(held, part, lax.rem(at + count - step, count), 0)
    return held


def contract_cols(left_side, right_side):
    return lax.dot_general(
        left_side, right_side, (((1,), (1,)), ((), ())), preferred_element_type=jnp.float32
    )


def combine(every):
    student_max = jnp.max(every[:, 0], axis=0)
    teacher_max = jnp.max(every[:, 1], axis=0)
    lower = every[:, 0] - student_max
    scale = jnp.exp(lower)
    return jnp.stack(
        [
            student_max,
            teacher_max,
            jnp.sum(every[:, 2] * scale, axis=0),
            jnp.sum((every[:, 3] + every[:, 2] * lower) * scale, axis=0),
            jnp.sum(every[:, 4] * scale, axis=0),
            jnp.sum(every[:, 5] * jnp.exp(every[:, 1] - teacher_max), axis=0),
            jnp.sum(every[:, 6], axis=0),
            jnp.zeros_like(student_max),
        ]
    )


def body(hidden, head_weight, teacher_logits, sampled_ids, behaviour_logprob, valid_mask):
    width_part, col_count = head_weight.shape
    sect, z_lo, x_at, z_hi, y_at = (lax.axis_index(name) for name in AXES)
    quarter = col_count // 4
    half = 4 * width_part
    f32, bf16 = jnp.float32, jnp.bfloat16

    piece = lax.dynamic_slice_in_dim(hidden, 64 * sect + 16 * x_at, 16, axis=0)
    far_piece = lax.ppermute(
        lax.dynamic_slice_in_dim(piece, half * (1 - z_hi), half, axis=1), "z_hi", PAIR
    )
    near_piece = lax.dynamic_slice_in_dim(piece, half * z_hi, half, axis=1)

    weight_parts = head_weight.T.reshape(4, quarter, width_part)

    def weight_for(step):
        return lax.dynamic_index_in_dim(weight_parts, lax.rem(y_at + step, 4), 0, keepdims=False)

    def logits_of(values):
        return sum(
            contract_cols(
                weight_half[k],
                lax.slice_in_dim(values, k * width_part, (k + 1) * width_part, axis=1),
            )
            for k in range(4)
        )

    def turned(values, axis):
        first, second = jnp.split(values, 2, axis=axis)
        return jnp.where(sect == 0, values, jnp.concatenate([second, first], axis=axis))

    pieces = spread(jnp.stack([far_piece, near_piece]), "y")
    mask = valid_mask.astype(f32)
    far_mask = lax.ppermute(mask, "z_hi", PAIR)
    sent = [weight_for(step) for step in (1, 2, 3)]
    pieces = spread(after(pieces, sent[0]), "x")
    weight_half = in_order(
        weight_for(0), [shift(values, "y", step) for step, values in enumerate(sent, 1)], y_at
    )
    other_pieces = lax.ppermute(pieces, "sect", PAIR)
    far_halves = [kept[:, :, 0].reshape(256, half) for kept in (pieces, other_pieces)]
    near_halves = [kept[:, :, 1].reshape(256, half) for kept in (pieces, other_pieces)]
    far_halves[1] = after(far_halves[1], far_mask)
    given_logits = [logits_of(values) for values in far_halves]
    far_logits = [lax.ppermute(values, "z_hi", PAIR) for values in given_logits]
    far_rows = jnp.concatenate(far_halves)
    near_rows = jnp.concatenate(near_halves)
    logits = jnp.concatenate(
        [
            logits_of(near_halves[0]) + after(far_logits[0], given_logits[1]),
            logits_of(near_halves[1]) + far_logits[1],
        ],
        axis=1,
    )

    teacher = lax.all_to_all(
        after(teacher_logits, given_logits[1]).reshape(64, 8, quarter).transpose(1, 0, 2),
        ("sect", "y"),
        0,
        0,
        tiled=True,
    )
    rows = jnp.stack(
        [sampled_ids.astype(f32), behaviour_logprob, mask, far_mask]
        + [jnp.zeros_like(behaviour_logprob)] * 4
    )
    rows = spread(after(rows, teacher), "y")
    valid_count = jnp.sum(rows[:, 2:4])
    rows = rows[:, :3].reshape(4, 3, 2, 4, 16).transpose(1, 2, 3, 0, 4)
    rows = turned(rows, 1).reshape(3, 512)
    ids, behaviour, valid = rows[0].astype(jnp.int32), rows[1], rows[2]

    teacher = teacher.reshape(2, 4, 4, 16, quarter)
    teacher = jnp.stack(
        [lax.dynamic_index_in_dim(teacher, at, 0, keepdims=False) for at in (sect, 1 - sect)]
    )
    teacher = teacher.transpose(0, 2, 1, 3, 4).reshape(512, quarter).T.astype(f32)

    first_col = (((z_lo * 4 + x_at) * 2 + sect) * 4 + y_at) * quarter
    matches = lax.broadcasted_iota(jnp.int32, logits.shape, 0) == ids - first_col
    own_max = jnp.max(logits, axis=0)
    own_teacher_max = jnp.max(teacher, axis=0)
    own_shifted = logits - own_max
    own_powers = jnp.exp(own_shifted)
    own = jnp.stack(
        [
            own_max,
            own_teacher_max,
            jnp.sum(own_powers, axis=0),
            jnp.sum(own_powers * own_shifted, axis=0),
            jnp.sum(own_powers * teacher, axis=0),
            jnp.sum(jnp.exp(teacher - own_teacher_max), axis=0),
            jnp.sum(jnp.where(matches, logits, 0.0), axis=0),
            jnp.zeros_like(own_max),
        ]
    )
    own = turned(own, 1)
    for axes in STAGES:
        own = combine(spread(own, axes))
    own = turned(own, 1)
    student_max, teacher_max, student_sum, shifted_sum, teacher_mix, teacher_sum, sampled_logit = (
        own[i] for i in range(7)
    )
    log_student = jnp.log(student_sum)
    student_lse = student_max + log_student
    teacher_lse = teacher_max + jnp.log(teacher_sum)
    entropy = log_student - shifted_sum / student_sum
    token_kl = shifted_sum / student_sum - log_student - teacher_mix / student_sum + teacher_lse
    ratio_weight = jnp.minimum(jnp.exp(sampled_logit - student_lse - behaviour), CLIP_RATIO)
    row_factor = valid * ratio_weight / valid_count
    near_grad = (
        row_factor
        * (jnp.exp(logits - student_max) / student_sum)
        * (logits - student_lse - (teacher - teacher_lse) - token_kl)
    ).astype(bf16)

    def own_rows(values):
        kept = turned(values.reshape(2, 4, 4, 16), 0)
        return lax.dynamic_index_in_dim(kept, y_at, axis=2, keepdims=False).reshape(128)

    cut = quarter // 2

    def product(step, grads, start=0):
        held = lax.dynamic_index_in_dim(
            weight_parts, lax.rem(y_at + step, 4), 0, keepdims=False
        )[start : start + grads.shape[0]]
        return lax.dot_general(
            grads, held, (((0,), (0,)), ((), ())), preferred_element_type=f32
        )

    def ring(values, ready=None):
        back, ahead = shift(values, "y", 1), shift(values, "y", 3)
        sent = (back[:cut], ahead[cut:])
        if ready is not None:
            sent = tuple(part + (ready[:cut, :512] * 0).astype(bf16) for part in sent)
        top, bottom = shift(sent[0], "y", 1), shift(sent[1], "y", 3)
        part = product(0, values) + product(3, back) + product(1, ahead)
        part = part + product(2, top) + product(2, bottom, cut)
        opposite = jnp.concatenate([top, bottom])
        return [values, back, opposite, ahead], opposite, part

    far_grad = lax.ppermute(near_grad, "z_hi", PAIR)
    near_all, near_last, near_part = ring(near_grad)
    far_all, _, far_part = ring(far_grad + near_last * 0, near_part)
    kept = jnp.stack([near_part[:256], far_part[:256]]) + lax.ppermute(
        jnp.stack([near_part[256:], far_part[256:]]), "sect", PAIR
    )
    kept = kept.reshape(2, 4, 4, 16, width_part).transpose(2, 1, 0, 3, 4)
    kept = kept.reshape(16, 32, width_part)
    sums = lax.all_to_all(kept, ("z_lo", "x"), 0, 0, tiled=True)
    sums = jnp.sum(sums, axis=0).astype(bf16)

    nothing = (kept[0, 0, 0] * 0).astype(bf16)
    near_all = in_order(near_all[0], near_all[1:], y_at, nothing)
    far_all = in_order(far_all[0], far_all[1:], y_at, nothing)

    token = lax.broadcasted_iota(jnp.int32, (128, 512), 0)
    place = ((token // 64 ^ sect) * 4 + token // 16 % 4) * 64 + y_at * 16 + token % 16
    chosen = (place == lax.broadcasted_iota(jnp.int32, (128, 512), 1)).astype(bf16)
    chosen = chosen + (kept[:4, :, :512].reshape(128, 512) * 0).astype(bf16)
    logit_grad = contract_cols(chosen, near_all.reshape(col_count, 512)).astype(bf16)

    def weight_part(rows_in, grads):
        held = lax.dynamic_slice_in_dim(rows_in, width_part * y_at, width_part, axis=1)
        held = held + (kept.reshape(512, width_part) * 0).astype(bf16)
        return jnp.dot(grads.reshape(col_count, 512), held, preferred_element_type=f32)

    weight_grad = (weight_part(near_rows, near_all) + weight_part(far_rows, far_all)).astype(bf16).T
    sums = sums + weight_grad[:32, :width_part] * 0 + logit_grad[:32, :width_part] * 0

    def handed_over(values, flip):
        moves = [
            ((j * 2 + z) * 4 + k, (k * 2 + (z ^ flip)) * 4 + j)
            for j in range(4)
            for z in range(2)
            for k in range(4)
        ]
        return lax.ppermute(values, ("z_lo", "z_hi", "y"), moves)

    near_sum, far_sum = handed_over(sums[:16], 0), handed_over(sums[16:], 1)
    both = jnp.where(
        z_hi == 0, jnp.concatenate([near_sum, far_sum]), jnp.concatenate([far_sum, near_sum])
    )
    mine = spread(both, ("z_lo", "x")).reshape(4, 4, 2, 16, width_part)
    mine = jnp.concatenate(
        [mine[k, :, z].reshape(64, width_part) for z in range(2) for k in range(4)], axis=1
    )
    hidden_grad = lax.dynamic_update_index_in_dim(
        jnp.stack([mine, mine]), lax.ppermute(mine, "sect", PAIR), 1 - sect, 0
    ).reshape(128, 8 * width_part)
    return (
        logit_grad,
        hidden_grad,
        weight_grad,
        own_rows(entropy),
        own_rows(token_kl),
    )


STAGES = (("sect", "x"), ("z_lo", "y"))


def solution(mesh):
    wide = Mesh(mesh.devices.reshape(SIZES), AXES)
    seq, vocab = ("z_hi", "y"), ("z_lo", "x")
    by_cols = P(seq, vocab + ("sect",))
    by_row = P(seq)
    return jax.shard_map(
        body,
        mesh=wide,
        in_specs=(P(seq, None), by_cols, P(seq + ("sect",), vocab), by_row, by_row, by_row),
        out_specs=(by_cols, P(seq, None), by_cols, by_row, by_row),
        check_vma=False,
    )
```
